128 devices in a mesh: grp: 4 (over z), blk: 32 (over y, x, core).
Axes of the slice: x: 4, y: 4, z: 4, core: 2. Of those that a mesh axis runs over, the one named last changes fastest.
Arguments:
- embeddings: bfloat16 [32768, 768], P(('grp', 'blk')), may hold values from -6 to 6
- target: int32 [32768, 1], P(('grp', 'blk')), may hold values from 0 to 127; in each aligned block of 256 rows (0 to 255, 256 to 511, ...) at most 4 rows name the same one
- cluster: int32 [32768], P(('grp', 'blk')), may hold values from 0 to 15
Outputs:
- nearest: float32 [32768], P(('grp', 'blk'))
The draws below stay inside these ranges and needn't reach their ends.
Inputs may be any that keep to these rules, and one draw needn't show every extreme that they name: The rows of one device send at most 4 rows to any one target.
All inputs are finite; a program needn't handle non-finite values.
Results may differ from the reference program's by a relative error of at most 0.0014.
Values may be sent and summed in bfloat16 or wider, within the bound.
A program may use at most 64 MiB of HBM per device.

```python
import math
import jax
import jax.numpy as jnp
import numpy as np
from jax import lax

D = 768
CLUSTERS = 64
ROWS_DEV = 256
ROWS = 32768
CAP = 4
N_GRP = 4
N_BLK = 32
DEVICES = 128


def place_ends(array, key, smallest, high):
    index_at = [jax.random.randint(jax.random.fold_in(key, axis), (), 0, length) for axis, length in enumerate(array.shape)]
    longest = array.shape.index(max(array.shape))
    beside = index_at[:longest] + [(index_at[longest] + 1) % array.shape[longest]] + index_at[longest + 1:]
    return array.at[tuple(index_at)].set(smallest).at[tuple(beside)].set(high)


def block_scale(rng, extent, cuts, low, largest):
    gain = 1.0
    for axis_at, parts in cuts:
        draws = jax.random.uniform(jax.random.fold_in(jax.random.fold_in(rng, 6), axis_at), (parts,), jnp.float32, low / len(cuts), largest / len(cuts))
        gain = gain * jnp.repeat(jnp.exp(draws), extent[axis_at] // parts).reshape((-1,) + (1,) * (len(extent) - 1 - axis_at))
    return gain


def cumulative_ranks(number_of, lean):
    loads = [(1 << 20) // math.isqrt(rank ** lean) + 1 for rank in range(1, number_of + 1)]
    deviation = 1 + sum(loads) // (1 << 30)
    return np.cumsum(np.array([max(1, weight // deviation) for weight in loads]))


def ranked_ids(stream_key, extent, count, slope):
    grid = cumulative_ranks(count, slope)
    pick = jax.random.randint(jax.random.fold_in(stream_key, 1), extent, 0, int(grid[count - 1]))
    standing = jnp.searchsorted(jnp.asarray(grid, jnp.int32), pick, side="right")
    return jax.random.permutation(jax.random.fold_in(stream_key, 2), count)[standing].astype(jnp.int32)


def assign_block(own_key, own, number, rows, count, top, limit, lean):
    sequence = jax.random.permutation(own_key, count)
    crowded, usual = load_shares(count, rows * top, limit, lean, True), load_shares(count, rows * top, limit, lean, False)
    places = jnp.arange(count)

    def named(tallies, offset_by):
        used = int((tallies > 0).sum())
        fixed = max(1, used // 4)
        passed = fixed + (places - fixed + offset_by * (used - fixed)) % max(1, count - fixed)
        return jnp.zeros((count,), jnp.int32).at[sequence[jnp.where(places < fixed, places, passed)]].set(jnp.asarray(tallies, jnp.int32))

    tallies = jnp.where(number % 4 == 0, named(crowded, number // 4), named(usual, number - number // 4 - 1))
    mixed = jax.random.permutation(jax.random.fold_in(own, 3), count)
    donor, taker = mixed[0:count // 2 * 2:2], mixed[1:count // 2 * 2:2]
    margin = jnp.minimum(tallies[donor] - 1, limit - tallies[taker]) // 2
    margin = jnp.where((donor == sequence[0]) | (taker == sequence[0]) | (tallies[taker] == 0), 0, jnp.maximum(margin, 0))
    passed = jax.random.randint(jax.random.fold_in(own, 4), (count // 2,), 0, 1 << 20) % (margin + 1)
    tallies = tallies.at[donor].add(-passed).at[taker].add(passed)
    items = jnp.searchsorted(jnp.cumsum(tallies), jnp.arange(rows * top), side="right").astype(jnp.int32)
    grid = items.reshape(top, rows).T
    grid = grid[jax.random.permutation(jax.random.fold_in(own, 1), rows)]
    offset_by = jax.random.randint(jax.random.fold_in(own, 2), (rows, 1), 0, top)
    return jnp.take_along_axis(grid, (jnp.arange(top)[None, :] + offset_by) % top, axis=1)


def load_shares(number_of, total, limit, slope, full):
    weights = [(1 << 20) // math.isqrt(grade ** slope) + 1 for grade in range(1, number_of + 1)]
    largest = limit if full else min(limit, max(-(-total // number_of), total * weights[0] // sum(weights)))
    least = 1 if total - largest >= number_of - 1 else 0
    given, surplus = [largest] + [least] * (number_of - 1), total - largest - least * (number_of - 1)
    while surplus > 0:
        free = [i for i in range(1, number_of) if given[i] < largest] or [i for i in range(1, number_of) if given[i] < limit]
        pool, remaining = sum([weights[i] for i in free]), surplus
        for i in free:
            extra = min(limit - given[i], max(1, remaining * weights[i] // pool), surplus)
            given[i] = given[i] + extra
            surplus = surplus - extra
    return np.array(given)


def noise(rng, shape, deviation, reach, shards=(), held_as=jnp.bfloat16):
    drawn = deviation * jax.random.normal(rng, shape, jnp.float32)
    if shards:
        drawn = drawn * block_scale(rng, shape, shards, -0.22, 0.18)
    return jnp.clip(drawn, -reach, reach).astype(held_as)


def setup_inputs(seed: int = 0) -> dict:
    splits = jax.random.split(jax.random.key(seed), 4)
    embeddings = noise(splits[0], (ROWS, D), 1.0, 6.0, ((0, 128),))
    target_keys = jax.random.split(jax.random.fold_in(splits[1], 1), ROWS // ROWS_DEV)
    target_turns = jax.random.permutation(jax.random.fold_in(splits[1], 3), ROWS // ROWS_DEV)
    target = jax.vmap(lambda own, number: assign_block(jax.random.fold_in(splits[1], 2), own, number, ROWS_DEV, DEVICES, 1, CAP, 2))(target_keys, target_turns).reshape((ROWS, 1))
    cluster = place_ends(ranked_ids(splits[2], (ROWS,), CLUSTERS // N_GRP, 2), jax.random.fold_in(splits[2], 3), 0, (CLUSTERS // N_GRP) - 1).astype(jnp.int32)
    return {"embeddings": embeddings, "target": target, "cluster": cluster}


def normalize(embeddings):
    widened = embeddings.astype(jnp.float32)
    scale_inv = lax.rsqrt(lax.optimization_barrier(jnp.sum(widened * widened, axis=1, keepdims=True)) + 1e-06)
    return (widened * scale_inv).astype(jnp.bfloat16)

def reference(embeddings, target, cluster):
    normed = normalize(embeddings)
    total = normed.shape[0]
    owner_key = target[:, 0] // N_BLK * CLUSTERS + cluster
    positions = jnp.arange(total, dtype=jnp.int32)
    block = math.gcd(total, 1024)

    def one_block(first):
        rows = lax.dynamic_slice_in_dim(normed, first, block, 0)
        keys = lax.dynamic_slice_in_dim(owner_key, first, block, 0)
        scores = jnp.dot(rows, normed.T, preferred_element_type=jnp.float32)
        row_pos = first + jnp.arange(block, dtype=jnp.int32)
        allowed = (keys[:, None] == owner_key[None, :]) & (row_pos[:, None] != positions[None, :])
        return lax.optimization_barrier(jnp.max(jnp.where(allowed, scores, -1.0), axis=1))
    firsts = jnp.arange(total // block, dtype=jnp.int32) * block
    return lax.map(one_block, firsts).reshape(total)
```

```python
import jax
import jax.numpy as jnp
from jax import lax
from jax.experimental import pallas as pl
from jax.experimental.pallas import tpu as pltpu
from jax.sharding import PartitionSpec as P

MESH = pl.DeviceIdType.MESH
LOWEST = -1.0
CHUNKS = 8
STOPS = (
    (0, 0, 0),
    (0, 2, 0),
    (1, 0, 2),
    (-1, 2, 0),
    (0, 0, 2),
    (1, 0, 1),
    (-1, -1, 0),
    (0, -1, 0),
    (0, 0, -1),
    (0, 1, 0),
    (-1, 0, 0),
    (1, 0, 0),
    (1, 0, -1),
)
SEND, WAIT, SEND_KEYS, WAIT_KEYS, TWIN, WAIT_TWIN, TWIN_KEYS, WAIT_TWIN_KEYS, PREPARE, COMPARE, FINISH = range(11)
TWINS = (0, 1, 3, 5, 6, 7, 8, 9, 10, 11)
PARTS = ((0, 1), (8, 0), (8, 1), (12, 0), (6, 0), (6, 1), (9, 0), (9, 1), (10, 0), (10, 1), (5, 0), (5, 1), (11, 0), (11, 1), (1, 0), (1, 1), (4, 0), (7, 0), (7, 1), (2, 0), (3, 0))
PROGRAM = (
    (TWIN_KEYS,),
    (SEND, 0, 0, 11, 0),
    (SEND, 0, 0, 10, 1),
    (SEND, 0, 0, 9, 2),
    (SEND, 0, 0, 8, 5),
    (SEND, 0, 0, 7, 3),
    (TWIN, 0),
    (WAIT_TWIN_KEYS,),
    (SEND_KEYS, 0, 11, 0),
    (SEND_KEYS, 0, 10, 1),
    (SEND_KEYS, 0, 9, 2),
    (SEND_KEYS, 0, 8, 5),
    (SEND_KEYS, 0, 7, 3),
    (PREPARE, 0),
    (WAIT_TWIN, 0),
    (COMPARE, 0, 0, 2, True, False),
    (SEND, 2, 0, 10, 1),
    (SEND, 3, 0, 8, 5),
    (SEND, 4, 0, 7, 3),
    (SEND, 1, 0, 11, 0),
    (SEND, 3, 0, 9, 2),
    (SEND, 2, 0, 7, 3),
    (SEND, 1, 0, 8, 5),
    (SEND, 5, 0, 11, 0),
    (SEND, 7, 0, 10, 1),
    (SEND, 7, 0, 9, 2),
    (WAIT, 11, 0),
    (WAIT, 10, 0),
    (WAIT, 9, 0),
    (WAIT, 8, 0),
    (WAIT, 7, 0),
    (SEND, 0, 11, 5, 4),
    (SEND, 1, 0, 7, 3),
    (SEND, 4, 0, 8, 5),
    (SEND, 4, 0, 11, 0),
    (SEND, 1, 0, 10, 1),
    (SEND, 1, 0, 9, 2),
    (WAIT, 10, 2),
    (WAIT, 8, 3),
    (WAIT, 7, 4),
    (WAIT, 11, 1),
    (WAIT, 9, 3),
    (SEND, 1, 11, 5, 4),
    (SEND, 3, 0, 7, 3),
    (SEND, 3, 0, 10, 1),
    (SEND, 2, 0, 11, 0),
    (SEND, 2, 0, 9, 2),
    (SEND, 2, 0, 8, 5),
    (WAIT, 7, 2),
    (WAIT, 8, 1),
    (WAIT, 11, 5),
    (WAIT, 10, 7),
    (WAIT, 9, 7),
    (SEND, 5, 11, 5, 4),
    (SEND, 5, 0, 7, 3),
    (SEND, 3, 0, 11, 0),
    (SEND, 6, 0, 10, 1),
    (SEND, 6, 0, 9, 2),
    (SEND, 5, 0, 8, 5),
    (WAIT, 5, 0),
    (WAIT, 7, 1),
    (WAIT, 8, 4),
    (WAIT, 11, 4),
    (WAIT, 10, 1),
    (WAIT, 9, 1),
    (SEND, 4, 11, 5, 4),
    (SEND, 7, 0, 7, 3),
    (SEND, 4, 0, 9, 2),
    (SEND, 4, 0, 10, 1),
    (SEND, 7, 0, 11, 0),
    (SEND, 6, 0, 8, 5),
    (WAIT, 5, 1),
    (WAIT, 7, 3),
    (WAIT, 10, 3),
    (WAIT, 11, 2),
    (WAIT, 9, 2),
    (WAIT, 8, 2),
    (SEND, 2, 11, 5, 4),
    (SEND, 6, 0, 7, 3),
    (SEND, 5, 0, 9, 2),
    (SEND, 6, 0, 11, 0),
    (SEND, 5, 0, 10, 1),
    (SEND, 7, 0, 8, 5),
    (WAIT, 5, 5),
    (WAIT, 7, 5),
    (WAIT, 11, 3),
    (WAIT, 10, 6),
    (WAIT, 9, 6),
    (WAIT, 8, 5),
    (SEND, 3, 11, 5, 4),
    (SEND, 0, 8, 12, 0),
    (SEND, 0, 7, 6, 1),
    (SEND, 2, 9, 1, 2),
    (SEND, 1, 11, 12, 5),
    (SEND, 1, 10, 6, 3),
    (WAIT, 5, 4),
    (WAIT, 7, 7),
    (WAIT, 9, 4),
    (WAIT, 10, 4),
    (WAIT, 11, 7),
    (WAIT, 8, 6),
    (SEND, 7, 11, 5, 4),
    (SEND, 1, 8, 4, 5),
    (SEND, 3, 7, 6, 1),
    (SEND, 0, 7, 1, 3),
    (SEND, 3, 9, 1, 2),
    (SEND, 2, 8, 12, 0),
    (WAIT, 5, 2),
    (WAIT, 7, 6),
    (TWIN, 7),
    (WAIT_KEYS, 7),
    (SEND_KEYS, 7, 6, 1),
    (SEND_KEYS, 7, 1, 3),
    (WAIT, 9, 5),
    (TWIN, 9),
    (WAIT_KEYS, 9),
    (WAIT, 11, 6),
    (TWIN, 11),
    (WAIT_KEYS, 11),
    (SEND_KEYS, 11, 5, 4),
    (WAIT, 10, 5),
    (TWIN, 10),
    (WAIT_KEYS, 10),
    (WAIT, 8, 7),
    (TWIN, 8),
    (WAIT_KEYS, 8),
    (SEND_KEYS, 8, 12, 0),
    (SEND_KEYS, 8, 4, 5),
    (SEND, 6, 11, 5, 4),
    (SEND, 0, 8, 4, 5),
    (SEND, 2, 10, 6, 3),
    (SEND, 1, 9, 1, 2),
    (SEND, 5, 7, 6, 1),
    (SEND, 6, 8, 12, 0),
    (PREPARE, 7),
    (COMPARE, 7, 0, 0, True, True),
    (PREPARE, 8),
    (COMPARE, 8, 0, 0, True, False),
    (WAIT, 5, 3),
    (WAIT, 12, 0),
    (WAIT, 6, 0),
    (WAIT, 1, 2),
    (WAIT, 12, 1),
    (WAIT, 6, 1),
    (SEND, 1, 5, 2, 4),
    (SEND, 3, 8, 4, 5),
    (SEND, 4, 7, 1, 3),
    (SEND, 6, 9, 1, 2),
    (SEND, 3, 8, 12, 0),
    (SEND, 6, 7, 6, 1),
    (PREPARE, 10),
    (COMPARE, 10, 0, 0, True, False),
    (FINISH, 0, True, True),
    (WAIT_TWIN, 8),
    (COMPARE, 7, 8, 0, False, True),
    (WAIT, 5, 7),
    (WAIT, 4, 1),
    (WAIT, 6, 3),
    (WAIT, 1, 0),
    (WAIT, 1, 3),
    (WAIT, 12, 2),
    (SEND, 2, 5, 2, 4),
    (SEND, 6, 8, 4, 5),
    (SEND, 7, 10, 6, 3),
    (SEND, 7, 9, 1, 2),
    (SEND, 7, 8, 12, 0),
    (SEND, 4, 7, 6, 1),
    (WAIT_TWIN, 9),
    (COMPARE, 7, 9, 1, False, False),
    (WAIT_TWIN, 10),
    (COMPARE, 7, 10, 0, False, True),
    (WAIT, 5, 6),
    (TWIN, 5),
    (WAIT_KEYS, 5),
    (SEND_KEYS, 5, 2, 4),
    (WAIT, 4, 0),
    (WAIT, 6, 2),
    (WAIT, 1, 1),
    (WAIT, 6, 5),
    (WAIT, 12, 6),
    (SEND, 0, 5, 2, 4),
    (SEND, 4, 8, 4, 5),
    (SEND, 5, 9, 1, 2),
    (SEND, 5, 8, 12, 0),
    (SEND, 1, 1, 3, 1),
    (SEND, 2, 6, 3, 3),
    (WAIT_TWIN, 11),
    (COMPARE, 7, 11, 0, False, True),
    (COMPARE, 8, 9, 0, False, True),
    (WAIT, 2, 1),
    (WAIT, 4, 3),
    (WAIT, 1, 4),
    (WAIT, 1, 6),
    (WAIT, 12, 3),
    (WAIT, 6, 6),
    (SEND, 5, 5, 2, 4),
    (SEND, 2, 8, 4, 5),
    (SEND, 4, 8, 12, 0),
    (SEND, 0, 6, 3, 3),
    (SEND, 3, 1, 3, 1),
    (COMPARE, 8, 10, 0, False, False),
    (COMPARE, 8, 11, 0, False, False),
    (WAIT, 2, 2),
    (COMPARE, 10, 11, 1, False, False),
    (WAIT, 4, 6),
    (WAIT, 6, 7),
    (WAIT, 1, 7),
    (WAIT, 12, 7),
    (WAIT, 6, 4),
    (TWIN, 6),
    (WAIT_KEYS, 6),
    (SEND_KEYS, 6, 3, 3),
    (SEND, 4, 5, 2, 4),
    (SEND, 5, 8, 4, 5),
    (SEND, 4, 6, 3, 3),
    (SEND, 3, 4, 2, 0),
    (SEND, 6, 1, 3, 1),
    (PREPARE, 5),
    (WAIT_TWIN, 7),
    (COMPARE, 5, 7, 0, True, True),
    (WAIT, 2, 0),
    (COMPARE, 5, 8, 0, False, False),
    (WAIT, 4, 4),
    (WAIT, 1, 5),
    (TWIN, 1),
    (WAIT_KEYS, 1),
    (WAIT, 12, 5),
    (WAIT, 3, 1),
    (WAIT, 3, 2),
    (SEND, 7, 5, 2, 4),
    (SEND, 7, 8, 4, 5),
    (SEND, 5, 6, 3, 3),
    (SEND, 6, 4, 2, 0),
    (SEND, 7, 1, 3, 1),
    (COMPARE, 5, 9, 0, False, False),
    (COMPARE, 5, 10, 0, False, False),
    (WAIT, 2, 5),
    (WAIT, 4, 2),
    (WAIT, 12, 4),
    (WAIT_KEYS, 12),
    (WAIT, 3, 0),
    (WAIT, 3, 3),
    (PREPARE, 6),
    (WAIT_TWIN, 5),
    (COMPARE, 6, 5, 0, True, True),
    (COMPARE, 6, 8, 0, False, False),
    (COMPARE, 6, 9, 0, False, False),
    (WAIT, 2, 4),
    (COMPARE, 6, 11, 0, False, False),
    (WAIT, 4, 5),
    (WAIT, 3, 4),
    (WAIT, 2, 3),
    (WAIT, 3, 6),
    (PREPARE, 1),
    (COMPARE, 1, 5, 0, True, False),
    (COMPARE, 1, 8, 0, False, False),
    (FINISH, 8, True, True),
    (PREPARE, 12),
    (WAIT_TWIN, 1),
    (COMPARE, 12, 1, 0, True, True),
    (WAIT, 2, 7),
    (WAIT, 4, 7),
    (WAIT_KEYS, 4),
    (WAIT, 3, 5),
    (WAIT, 2, 6),
    (WAIT_KEYS, 2),
    (WAIT, 3, 7),
    (TWIN, 3),
    (WAIT_KEYS, 3),
    (COMPARE, 12, 5, 1, False, False),
    (WAIT_TWIN, 6),
    (COMPARE, 12, 6, 0, False, True),
    (COMPARE, 12, 9, 0, False, False),
    (FINISH, 12, True, False),
    (PREPARE, 2),
    (COMPARE, 2, 1, 0, True, False),
    (COMPARE, 2, 6, 0, False, False),
    (FINISH, 6, True, True),
    (COMPARE, 2, 7, 0, False, False),
    (COMPARE, 2, 9, 0, False, False),
    (FINISH, 9, False, True),
    (COMPARE, 2, 10, 1, False, False),
    (FINISH, 10, True, True),
    (PREPARE, 3),
    (COMPARE, 3, 5, 0, True, False),
    (FINISH, 5, True, True),
    (COMPARE, 3, 11, 1, False, False),
    (FINISH, 11, False, True),
    (PREPARE, 4),
    (COMPARE, 4, 1, 1, True, False),
    (FINISH, 1, True, True),
    (COMPARE, 4, 7, 0, False, False),
    (FINISH, 4, True, False),
    (FINISH, 7, True, True),
    (WAIT_TWIN, 3),
    (COMPARE, 2, 3, 1, False, False),
    (FINISH, 2, True, False),
    (FINISH, 3, True, False),
)
STEPS_IN = ((1, 0, 0), (-1, 0, 0), (0, 1, 0), (0, -1, 0), (0, 0, 1), (0, 0, -1))
COUNT = len(STOPS)


def at_offset(offset, other_core):
    z, blk = lax.axis_index("grp"), lax.axis_index("blk")
    core, x, y = blk % 2, blk // 2 % 4, blk // 8
    if other_core:
        core = 1 - core
    x, y, z = (x + offset[0] + 4) % 4, (y + offset[1] + 4) % 4, (z + offset[2] + 4) % 4
    return (z, (y * 4 + x) * 2 + core)


def kernel(
    x_ref, target_ref, cluster_ref, out_ref,
    rows, keys, key_cols, row_max, col_max, parts, heard,
    row_sent, row_got, key_sent, key_got, twin_sent, twin_got, twin_key, part_sent, part_got,
):
    size, width = x_ref.shape
    piece = size // CHUNKS
    here = (0, 0, 0)
    barrier = pltpu.get_barrier_semaphore()
    near = [at_offset(step, False) for step in STEPS_IN] + [at_offset(here, True)]
    for device in near:
        pl.semaphore_signal(barrier, inc=1, device_id=device, device_id_type=MESH)

    key = jnp.right_shift(target_ref[...], 5) * 64 + cluster_ref[...]
    keys[0, 0] = key.astype(jnp.float32)

    def normalize(part):
        here_rows = pl.ds(part * piece, piece)
        wide = x_ref[here_rows].astype(jnp.float32)
        scale_inv = lax.rsqrt(jnp.sum(wide * wide, axis=1, keepdims=True) + 1e-06)
        rows[0, 0, here_rows] = (wide * scale_inv).astype(jnp.bfloat16)

    for part in range(CHUNKS):
        normalize(part)
    pl.semaphore_wait(barrier, len(near))

    def remote(src, dst, sent, got, device):
        return pltpu.make_async_remote_copy(
            src_ref=src, dst_ref=dst, send_sem=sent, recv_sem=got, device_id=device, device_id_type=MESH
        )

    def send_rows(part, src, dst, step):
        here_rows = pl.ds(part * piece, piece)
        return remote(
            rows.at[src, 0, here_rows], rows.at[dst, 0, here_rows],
            row_sent.at[dst], row_got.at[dst, part], at_offset(STEPS_IN[step], False),
        )

    def send_keys(src, dst, step):
        return remote(
            keys.at[src], keys.at[dst], key_sent.at[dst], key_got.at[dst], at_offset(STEPS_IN[step], False)
        )

    def to_twin(slot):
        return remote(
            rows.at[slot, 0], rows.at[slot, 1], twin_sent.at[slot], twin_got.at[slot], at_offset(here, True)
        )

    def keys_to_twin():
        return remote(
            keys.at[0, 0], keys.at[0, 1], twin_key.at[0], twin_key.at[1], at_offset(here, True)
        )

    def send_part(slot, half):
        offset = tuple(-v for v in STOPS[slot])
        return remote(
            parts.at[slot, half], heard.at[slot, half],
            part_sent.at[slot, half], part_got.at[slot, half], at_offset(offset, half == 1),
        )

    def prepare(slot):
        spread = jnp.broadcast_to(keys[slot, 0], (128, size))
        key_cols[slot] = spread.T

    def compare(left, right, mode, fresh_row, fresh_col):
        best_row = None
        for half in range(2):
            scores = lax.dot_general(
                rows[left, 0], rows[right, half], (((1,), (1,)), ((), ())), preferred_element_type=jnp.float32
            )
            allowed = []
            for lane in range(0, size, 128):
                same = key_cols[left] == keys[right, half][:, lane : lane + 128]
                if mode == 2 and half == 0:
                    row_at = lax.broadcasted_iota(jnp.int32, (size, 128), 0)
                    col_at = lax.broadcasted_iota(jnp.int32, (size, 128), 1) + lane
                    same = same & (row_at != col_at)
                block = jnp.where(same, scores[:, lane : lane + 128], LOWEST)
                best_row = block if best_row is None else jnp.maximum(best_row, block)
                if mode == 0:
                    best = jnp.max(block.reshape(size // 8, 8, 128), axis=0)
                    place = (right, half, slice(None), slice(lane, lane + 128))
                    col_max[place] = best if fresh_col else jnp.maximum(col_max[place], best)
        row_max[left] = best_row if fresh_row else jnp.maximum(row_max[left], best_row)

    def finish(slot, has_row, has_col):
        best = None
        if has_row:
            best = jnp.max(row_max[slot].T, axis=0, keepdims=True)
        if has_col:
            col = jnp.max(col_max[slot, 0], axis=0, keepdims=True)
            best = col if best is None else jnp.maximum(best, col)
            parts[slot, 1] = jnp.max(col_max[slot, 1], axis=0, keepdims=True)
        parts[slot, 0] = best
        if slot or has_col:
            for half in range(2):
                if (slot or half) and (half == 0 or has_col):
                    send_part(slot, half).start()

    started = []
    for op, *args in PROGRAM:
        if op == SEND:
            send_rows(*args).start()
        elif op == WAIT:
            slot, part = args
            send_rows(part, 0, slot, 0).wait_recv()
        elif op == SEND_KEYS:
            send_keys(*args).start()
        elif op == WAIT_KEYS:
            send_keys(0, args[0], 0).wait_recv()
        elif op == TWIN:
            to_twin(args[0]).start()
        elif op == WAIT_TWIN:
            to_twin(args[0]).wait_recv()
        elif op == TWIN_KEYS:
            keys_to_twin().start()
        elif op == WAIT_TWIN_KEYS:
            keys_to_twin().wait_recv()
        elif op == PREPARE:
            prepare(*args)
        elif op == COMPARE:
            compare(*args)
        elif op == FINISH:
            finish(*args)

    for slot in range(1, COUNT):
        remote(rows.at[0, 0], rows.at[slot, 0], row_sent.at[slot], row_got.at[slot, 0], near[0]).wait_send()
        send_keys(0, slot, 0).wait_send()
    for slot in TWINS:
        to_twin(slot).wait_send()
    keys_to_twin().wait_send()
    best = parts[0, 0]
    for slot, half in PARTS:
        send_part(slot, half).wait_recv()
        best = jnp.maximum(best, heard[slot, half])
    for slot, half in PARTS:
        send_part(slot, half).wait_send()
    out_ref[...] = best


def body(embeddings, target, cluster):
    size, width = embeddings.shape
    vmem = pl.BlockSpec(memory_space=pltpu.VMEM)
    dma = pltpu.SemaphoreType.DMA
    best = pl.pallas_call(
        kernel,
        out_shape=jax.ShapeDtypeStruct((1, size), jnp.float32),
        in_specs=[vmem] * 3,
        out_specs=vmem,
        scratch_shapes=[
            pltpu.VMEM((COUNT, 2, size, width), jnp.bfloat16),
            pltpu.VMEM((COUNT, 2, 1, size), jnp.float32),
            pltpu.VMEM((COUNT, size, 128), jnp.float32),
            pltpu.VMEM((COUNT, size, 128), jnp.float32),
            pltpu.VMEM((COUNT, 2, 8, size), jnp.float32),
            pltpu.VMEM((COUNT, 2, 1, size), jnp.float32),
            pltpu.VMEM((COUNT, 2, 1, size), jnp.float32),
            dma((COUNT,)), dma((COUNT, CHUNKS)), dma((COUNT,)), dma((COUNT,)), dma((COUNT,)), dma((COUNT,)),
            dma((2,)), dma((COUNT, 2)), dma((COUNT, 2)),
        ],
        compiler_params=pltpu.CompilerParams(
            collective_id=0, has_side_effects=True, vmem_limit_bytes=48 * 2**20
        ),
        name="nearest",
    )(embeddings, target.reshape(1, size), cluster.reshape(1, size))
    return best.reshape(size)


def solution(mesh):
    return jax.shard_map(
        body,
        mesh=mesh,
        in_specs=(P(("grp", "blk"), None), P(("grp", "blk"), None), P(("grp", "blk"))),
        out_specs=P(("grp", "blk")),
        check_vma=False,
    )
```

```python
import jax
import jax.numpy as jnp
from jax import lax
from jax.experimental import pallas as pl
from jax.experimental.pallas import tpu as pltpu
from jax.sharding import PartitionSpec as P

MESH = pl.DeviceIdType.MESH
LOWEST = -1.0
CUTS = ((0, 64), (64, 64), (128, 128))
CHUNKS = len(CUTS)
STOPS = (
    (0, 0, 0),
    (0, 2, 0),
    (1, 0, 0),
    (0, 0, 2),
    (1, 2, 0),
    (-1, 0, -1),
    (-1, 0, 1),
    (0, 0, -1),
    (0, 1, 0),
    (-1, 0, 2),
    (1, -1, 0),
    (-1, 0, 0),
    (0, -1, 0),
)
(
    ENTER, NORMALIZE, OWN_KEYS, SEND, WAIT, SEND_KEYS, WAIT_KEYS, TWIN, WAIT_TWIN, TWIN_KEYS, WAIT_TWIN_KEYS, PREPARE, COMPARE, FINISH_ROWS, FINISH_COLS, TELL, HEAR, DRAIN, DRAIN_TWIN, DRAIN_TWIN_KEYS, DRAIN_TELL,
) = range(21)
PROGRAM = (
    (NORMALIZE, 0), (ENTER,), (SEND, 0, 0, 12, 3), (SEND, 0, 0, 7, 5), (SEND, 0, 0, 11, 1), (SEND, 0, 0, 8, 2),
    (SEND, 0, 0, 2, 0), (OWN_KEYS,), (TWIN_KEYS,), (TWIN, 0, 0), (NORMALIZE, 1), (TWIN, 0, 1), (NORMALIZE, 2),
    (TWIN, 0, 2), (WAIT_TWIN_KEYS,), (SEND_KEYS, 0, 12, 3), (SEND_KEYS, 0, 7, 5), (SEND_KEYS, 0, 11, 1),
    (SEND_KEYS, 0, 8, 2), (SEND_KEYS, 0, 2, 0), (PREPARE, 0), (WAIT_TWIN, 0), (COMPARE, 0, 0, 2, True, True),
    (FINISH_ROWS, 0), (SEND, 1, 0, 11, 1), (SEND, 1, 0, 12, 3), (SEND, 1, 0, 8, 2), (SEND, 2, 0, 2, 0),
    (SEND, 2, 0, 7, 5), (WAIT, 12, 0), (TWIN, 12, 0), (WAIT_KEYS, 12), (SEND_KEYS, 12, 10, 0), (PREPARE, 12),
    (WAIT, 7, 0), (TWIN, 7, 0), (WAIT_KEYS, 7), (SEND_KEYS, 7, 5, 1), (SEND_KEYS, 7, 3, 5), (PREPARE, 7),
    (WAIT, 11, 0), (TWIN, 11, 0), (WAIT_KEYS, 11), (SEND_KEYS, 11, 6, 4), (PREPARE, 11), (WAIT, 8, 0), (TWIN, 8, 0),
    (WAIT_KEYS, 8), (SEND_KEYS, 8, 1, 2), (PREPARE, 8), (WAIT, 2, 0), (WAIT_KEYS, 2), (PREPARE, 2),
    (SEND, 0, 11, 6, 4), (SEND, 0, 7, 5, 1), (SEND, 0, 8, 1, 2), (SEND, 2, 0, 12, 3), (WAIT, 11, 1), (TWIN, 11, 1),
    (WAIT, 12, 1), (TWIN, 12, 1), (WAIT, 8, 1), (TWIN, 8, 1), (SEND, 1, 11, 6, 4), (SEND, 2, 0, 11, 1),
    (SEND, 0, 12, 10, 0), (SEND, 1, 11, 5, 5), (SEND, 2, 0, 8, 2), (WAIT, 6, 0), (TWIN, 6, 0), (WAIT_KEYS, 6),
    (SEND_KEYS, 6, 9, 4), (PREPARE, 6), (WAIT, 2, 2), (WAIT, 7, 2), (TWIN, 7, 2), (WAIT, 5, 0), (TWIN, 5, 0),
    (WAIT_KEYS, 5), (PREPARE, 5), (WAIT, 1, 0), (WAIT_KEYS, 1), (SEND_KEYS, 1, 4, 0), (PREPARE, 1),
    (SEND, 0, 6, 9, 4), (SEND, 0, 1, 4, 0), (SEND, 2, 7, 3, 5), (SEND, 2, 2, 10, 3), (WAIT, 6, 1), (TWIN, 6, 1),
    (WAIT, 12, 2), (TWIN, 12, 2), (WAIT, 10, 0), (TWIN, 10, 0), (WAIT_KEYS, 10), (PREPARE, 10), (WAIT, 5, 1),
    (TWIN, 5, 1), (SEND, 1, 6, 9, 4), (SEND, 1, 5, 7, 0), (SEND, 1, 8, 1, 2), (SEND, 2, 7, 5, 1),
    (COMPARE, 12, 0, 0, True, True), (FINISH_ROWS, 12), (WAIT, 9, 0), (TWIN, 9, 0), (WAIT_KEYS, 9), (PREPARE, 9),
    (WAIT, 11, 2), (TWIN, 11, 2), (WAIT, 8, 2), (TWIN, 8, 2), (WAIT, 4, 0), (TWIN, 4, 0), (WAIT_KEYS, 4),
    (PREPARE, 4), (SEND, 2, 11, 6, 4), (SEND, 0, 7, 3, 5), (SEND, 1, 12, 10, 0), (SEND, 2, 8, 1, 2),
    (COMPARE, 11, 0, 0, True, False), (WAIT_TWIN, 12), (COMPARE, 11, 12, 0, False, True),
    (COMPARE, 8, 12, 1, True, False), (FINISH_ROWS, 8), (WAIT_TWIN, 8), (COMPARE, 11, 8, 0, False, True),
    (FINISH_ROWS, 11), (WAIT, 9, 1), (TWIN, 9, 1), (WAIT, 3, 2), (TWIN, 3, 2), (WAIT, 10, 2), (TWIN, 10, 2),
    (SEND, 2, 10, 4, 3), (WAIT, 7, 1), (TWIN, 7, 1), (WAIT, 1, 1), (SEND, 1, 7, 3, 5), (SEND, 1, 1, 4, 0),
    (SEND, 2, 3, 9, 1), (COMPARE, 7, 12, 0, True, False), (COMPARE, 7, 8, 0, False, False),
    (COMPARE, 7, 0, 0, False, False), (WAIT_TWIN, 11), (COMPARE, 7, 11, 0, False, True), (FINISH_ROWS, 7),
    (WAIT, 3, 0), (TWIN, 3, 0), (WAIT_KEYS, 3), (PREPARE, 3), (WAIT, 5, 2), (TWIN, 5, 2), (WAIT, 10, 1),
    (TWIN, 10, 1), (SEND, 1, 10, 2, 2), (COMPARE, 5, 12, 0, True, False), (COMPARE, 5, 8, 0, False, False),
    (COMPARE, 5, 0, 0, False, False), (COMPARE, 10, 8, 0, True, False), (COMPARE, 10, 11, 0, False, False),
    (FINISH_ROWS, 10), (FINISH_COLS, 11, True), (TELL, 11, 0), (TELL, 11, 1), (WAIT_TWIN, 10),
    (COMPARE, 5, 10, 0, False, True), (FINISH_ROWS, 5), (WAIT, 6, 2), (TWIN, 6, 2), (WAIT, 1, 2), (WAIT, 3, 1),
    (TWIN, 3, 1), (WAIT, 4, 1), (TWIN, 4, 1), (WAIT_TWIN, 7), (COMPARE, 6, 7, 0, True, True),
    (COMPARE, 6, 10, 0, False, False), (COMPARE, 6, 12, 0, False, False), (FINISH_COLS, 12, True), (TELL, 12, 0),
    (TELL, 12, 1), (COMPARE, 6, 8, 0, False, False), (FINISH_ROWS, 6), (COMPARE, 3, 8, 0, True, False),
    (COMPARE, 3, 10, 0, False, False), (FINISH_ROWS, 3), (COMPARE, 1, 7, 0, True, False), (FINISH_COLS, 7, True),
    (TELL, 7, 0), (TELL, 7, 1), (WAIT_TWIN, 5), (COMPARE, 1, 5, 0, False, True), (FINISH_COLS, 5, True), (TELL, 5, 0),
    (TELL, 5, 1), (WAIT, 4, 2), (TWIN, 4, 2), (WAIT, 2, 1), (WAIT, 9, 2), (TWIN, 9, 2), (WAIT_TWIN, 6),
    (COMPARE, 4, 6, 0, True, True), (COMPARE, 4, 11, 1, False, False), (WAIT_TWIN, 3),
    (COMPARE, 4, 3, 0, False, True), (FINISH_COLS, 3, True), (TELL, 3, 0), (TELL, 3, 1), (FINISH_ROWS, 4),
    (TELL, 4, 0), (COMPARE, 9, 8, 0, True, False), (FINISH_COLS, 8, True), (TELL, 8, 0), (TELL, 8, 1),
    (COMPARE, 9, 10, 0, False, False), (FINISH_COLS, 10, True), (TELL, 10, 0), (TELL, 10, 1), (WAIT_TWIN, 4),
    (COMPARE, 9, 4, 1, False, True), (FINISH_ROWS, 9), (TELL, 9, 0), (COMPARE, 1, 6, 0, False, False),
    (COMPARE, 1, 3, 1, False, False), (FINISH_ROWS, 1), (TELL, 1, 0), (COMPARE, 2, 6, 0, True, False),
    (FINISH_COLS, 6, True), (TELL, 6, 0), (TELL, 6, 1), (COMPARE, 2, 11, 1, False, False), (WAIT_TWIN, 9),
    (COMPARE, 2, 9, 1, False, True), (FINISH_ROWS, 2), (TELL, 2, 0), (COMPARE, 3, 0, 3, False, False),
    (FINISH_COLS, 0, True), (TELL, 0, 1), (DRAIN, 1), (DRAIN, 2), (DRAIN, 3), (DRAIN, 4), (DRAIN, 5), (DRAIN, 6),
    (DRAIN, 7), (DRAIN, 8), (DRAIN, 9), (DRAIN, 10), (DRAIN, 11), (DRAIN, 12), (DRAIN_TWIN, 0), (DRAIN_TWIN, 3),
    (DRAIN_TWIN, 4), (DRAIN_TWIN, 5), (DRAIN_TWIN, 6), (DRAIN_TWIN, 7), (DRAIN_TWIN, 8), (DRAIN_TWIN, 9),
    (DRAIN_TWIN, 10), (DRAIN_TWIN, 11), (DRAIN_TWIN, 12), (DRAIN_TWIN_KEYS,), (HEAR, 11, 0), (HEAR, 11, 1),
    (HEAR, 12, 0), (HEAR, 12, 1), (HEAR, 7, 0), (HEAR, 7, 1), (HEAR, 5, 0), (HEAR, 5, 1), (HEAR, 3, 0), (HEAR, 3, 1),
    (HEAR, 4, 0), (HEAR, 8, 0), (HEAR, 8, 1), (HEAR, 10, 0), (HEAR, 10, 1), (HEAR, 9, 0), (HEAR, 1, 0), (HEAR, 6, 0),
    (HEAR, 6, 1), (HEAR, 2, 0), (HEAR, 0, 1), (DRAIN_TELL, 11, 0), (DRAIN_TELL, 11, 1), (DRAIN_TELL, 12, 0),
    (DRAIN_TELL, 12, 1), (DRAIN_TELL, 7, 0), (DRAIN_TELL, 7, 1), (DRAIN_TELL, 5, 0), (DRAIN_TELL, 5, 1),
    (DRAIN_TELL, 3, 0), (DRAIN_TELL, 3, 1), (DRAIN_TELL, 4, 0), (DRAIN_TELL, 8, 0), (DRAIN_TELL, 8, 1),
    (DRAIN_TELL, 10, 0), (DRAIN_TELL, 10, 1), (DRAIN_TELL, 9, 0), (DRAIN_TELL, 1, 0), (DRAIN_TELL, 6, 0),
    (DRAIN_TELL, 6, 1), (DRAIN_TELL, 2, 0), (DRAIN_TELL, 0, 1),
)
BOTH, ROWS, OWN, COLS = range(4)
STEPS_IN = ((1, 0, 0), (-1, 0, 0), (0, 1, 0), (0, -1, 0), (0, 0, 1), (0, 0, -1))
COUNT = len(STOPS)


def at_offset(offset, other_core):
    z, blk = lax.axis_index("grp"), lax.axis_index("blk")
    core, x, y = blk % 2, blk // 2 % 4, blk // 8
    if other_core:
        core = 1 - core
    x, y, z = (x + offset[0] + 4) % 4, (y + offset[1] + 4) % 4, (z + offset[2] + 4) % 4
    return (z, (y * 4 + x) * 2 + core)


def kernel(
    x_hbm, target_hbm, cluster_hbm, out_ref,
    raw, target, cluster, rows, keys, key_cols, row_max, col_max, parts, heard,
    copied, row_sent, row_got, key_sent, key_got, twin_sent, twin_got, twin_key, part_sent, part_got,
):
    size = raw.shape[0]
    here = (0, 0, 0)
    def piece(part):
        return pl.ds(CUTS[part][0], CUTS[part][1])

    def load(part):
        return pltpu.make_async_copy(x_hbm.at[piece(part)], raw.at[piece(part)], copied.at[part])

    load_target = pltpu.make_async_copy(target_hbm, target, copied.at[CHUNKS])
    load_cluster = pltpu.make_async_copy(cluster_hbm, cluster, copied.at[CHUNKS + 1])
    for part in range(CHUNKS):
        load(part).start()
    load_target.start()
    load_cluster.start()

    barrier = pltpu.get_barrier_semaphore()
    near = [at_offset(step, False) for step in STEPS_IN] + [at_offset(here, True)]
    for device in near:
        pl.semaphore_signal(barrier, inc=1, device_id=device, device_id_type=MESH)

    def normalize(part):
        load(part).wait()
        wide = raw[piece(part)].astype(jnp.float32)
        scale_inv = lax.rsqrt(jnp.sum(wide * wide, axis=1, keepdims=True) + 1e-06)
        rows[0, 0, piece(part)] = (wide * scale_inv).astype(jnp.bfloat16)

    def own_keys():
        load_target.wait()
        load_cluster.wait()
        key = jnp.right_shift(target[...], 5) * 64 + cluster[...]
        keys[0, 0] = key.astype(jnp.float32)

    def remote(src, dst, sent, got, device):
        return pltpu.make_async_remote_copy(
            src_ref=src, dst_ref=dst, send_sem=sent, recv_sem=got, device_id=device, device_id_type=MESH
        )

    def send_rows(part, src, dst, step):
        return remote(
            rows.at[src, 0, piece(part)], rows.at[dst, 0, piece(part)],
            row_sent.at[dst], row_got.at[dst, part], near[step],
        )

    def send_keys(src, dst, step):
        return remote(keys.at[src], keys.at[dst], key_sent.at[dst], key_got.at[dst], near[step])

    def to_twin(slot, where):
        return remote(rows.at[slot, 0, where], rows.at[slot, 1, where], twin_sent.at[slot], twin_got.at[slot], near[6])

    def keys_to_twin():
        return remote(keys.at[0, 0], keys.at[0, 1], twin_key.at[0], twin_key.at[1], near[6])

    def send_part(slot, half):
        offset = tuple(-v for v in STOPS[slot])
        return remote(
            parts.at[slot, half], heard.at[slot, half],
            part_sent.at[slot, half], part_got.at[slot, half], at_offset(offset, half == 1),
        )

    def prepare(slot):
        spread = jnp.broadcast_to(keys[slot, 0], (128, size))
        key_cols[slot] = spread.T

    def compare(left, right, mode, fresh_row, fresh_col):
        best_row = None
        for half in range(2):
            scores = lax.dot_general(
                rows[left, 0], rows[right, half], (((1,), (1,)), ((), ())), preferred_element_type=jnp.float32
            )
            for lane in range(0, size, 128):
                same = key_cols[left] == keys[right, half][:, lane : lane + 128]
                if mode == OWN and half == 0:
                    row_at = lax.broadcasted_iota(jnp.int32, (size, 128), 0)
                    col_at = lax.broadcasted_iota(jnp.int32, (size, 128), 1) + lane
                    same = same & (row_at != col_at)
                block = jnp.where(same, scores[:, lane : lane + 128], LOWEST)
                if mode != COLS:
                    best_row = block if best_row is None else jnp.maximum(best_row, block)
                if mode in (BOTH, COLS):
                    best = jnp.max(block.reshape(size // 8, 8, 128), axis=0)
                    place = (right, half, slice(None), slice(lane, lane + 128))
                    col_max[place] = best if fresh_col else jnp.maximum(col_max[place], best)
        if mode != COLS:
            row_max[left] = best_row if fresh_row else jnp.maximum(row_max[left], best_row)

    def finish_rows(slot):
        parts[slot, 0] = jnp.max(row_max[slot].T, axis=0, keepdims=True)

    def finish_cols(slot, add):
        col = jnp.max(col_max[slot, 0], axis=0, keepdims=True)
        parts[slot, 0] = jnp.maximum(parts[slot, 0], col) if add else col
        parts[slot, 1] = jnp.max(col_max[slot, 1], axis=0, keepdims=True)

    def drain(slot):
        remote(rows.at[0, 0], rows.at[slot, 0], row_sent.at[slot], row_got.at[slot, 0], near[0]).wait_send()
        send_keys(0, slot, 0).wait_send()

    whole = pl.ds(0, size)

    def run(program):
        best = None
        for op, *args in program:
            if op == ENTER:
                pl.semaphore_wait(barrier, len(near))
            elif op == NORMALIZE:
                normalize(*args)
            elif op == OWN_KEYS:
                own_keys()
            elif op == SEND:
                send_rows(*args).start()
            elif op == WAIT:
                send_rows(args[1], 0, args[0], 0).wait_recv()
            elif op == SEND_KEYS:
                send_keys(*args).start()
            elif op == WAIT_KEYS:
                send_keys(0, args[0], 0).wait_recv()
            elif op == TWIN:
                to_twin(args[0], piece(args[1])).start()
            elif op == WAIT_TWIN:
                to_twin(args[0], whole).wait_recv()
            elif op == TWIN_KEYS:
                keys_to_twin().start()
            elif op == WAIT_TWIN_KEYS:
                keys_to_twin().wait_recv()
            elif op == PREPARE:
                prepare(*args)
            elif op == COMPARE:
                compare(*args)
            elif op == FINISH_ROWS:
                finish_rows(*args)
            elif op == FINISH_COLS:
                finish_cols(*args)
            elif op == TELL:
                send_part(*args).start()
            elif op == HEAR:
                send_part(*args).wait_recv()
                news = heard[args[0], args[1]]
                best = news if best is None else jnp.maximum(best, news)
            elif op == DRAIN:
                drain(*args)
            elif op == DRAIN_TWIN:
                to_twin(args[0], whole).wait_send()
            elif op == DRAIN_TWIN_KEYS:
                keys_to_twin().wait_send()
            elif op == DRAIN_TELL:
                send_part(*args).wait_send()
        out_ref[...] = jnp.maximum(best, parts[0, 0])

    run(PROGRAM)


def body(embeddings, target, cluster):
    size, width = embeddings.shape
    hbm, vmem = pl.BlockSpec(memory_space=pltpu.HBM), pl.BlockSpec(memory_space=pltpu.VMEM)
    dma = pltpu.SemaphoreType.DMA
    best = pl.pallas_call(
        kernel,
        out_shape=jax.ShapeDtypeStruct((1, size), jnp.float32),
        in_specs=[hbm] * 3,
        out_specs=vmem,
        scratch_shapes=[
            pltpu.VMEM((size, width), jnp.bfloat16),
            pltpu.VMEM((1, size), jnp.int32),
            pltpu.VMEM((1, size), jnp.int32),
            pltpu.VMEM((COUNT, 2, size, width), jnp.bfloat16),
            pltpu.VMEM((COUNT, 2, 1, size), jnp.float32),
            pltpu.VMEM((COUNT, size, 128), jnp.float32),
            pltpu.VMEM((COUNT, size, 128), jnp.float32),
            pltpu.VMEM((COUNT, 2, 8, size), jnp.float32),
            pltpu.VMEM((COUNT, 2, 1, size), jnp.float32),
            pltpu.VMEM((COUNT, 2, 1, size), jnp.float32),
            dma((CHUNKS + 2,)), dma((COUNT,)), dma((COUNT, CHUNKS)), dma((COUNT,)), dma((COUNT,)),
            dma((COUNT,)), dma((COUNT,)), dma((2,)), dma((COUNT, 2)), dma((COUNT, 2)),
        ],
        compiler_params=pltpu.CompilerParams(
            collective_id=0, has_side_effects=True, vmem_limit_bytes=56553472
        ),
        name="nearest",
    )(embeddings, target.reshape(1, size), cluster.reshape(1, size))
    return best.reshape(size)


def solution(mesh):
    return jax.shard_map(
        body,
        mesh=mesh,
        in_specs=(P(("grp", "blk"), None), P(("grp", "blk"), None), P(("grp", "blk"))),
        out_specs=P(("grp", "blk")),
        check_vma=False,
    )
```

```python
import jax
import jax.numpy as jnp
from jax import lax
from jax.experimental import pallas as pl
from jax.experimental.pallas import tpu as pltpu
from jax.sharding import PartitionSpec as P

MESH = pl.DeviceIdType.MESH
LOWEST = -1.0
CUTS = ((0, 64), (64, 96), (160, 96))
CHUNKS = len(CUTS)
STOPS = (
    (0, 0, 0),
    (0, 2, 1),
    (2, 0, 0),
    (0, 1, 0),
    (-1, 0, -1),
    (0, 0, -1),
    (0, -1, 1),
    (0, 0, 1),
    (0, 2, 0),
    (-1, 0, 0),
    (2, 0, -1),
    (0, -1, 0),
    (1, 0, -1),
)
(
    ENTER, NORMALIZE, OWN_KEYS, SEND, WAIT, SEND_KEYS, WAIT_KEYS, TWIN, WAIT_TWIN, TWIN_KEYS, WAIT_TWIN_KEYS, PREPARE, COMPARE, FINISH_ROWS, FINISH_COLS, TELL, HEAR, DRAIN, DRAIN_TWIN, DRAIN_TWIN_KEYS, DRAIN_TELL,
) = range(21)
PROGRAM = (
    (NORMALIZE, 0), (ENTER,), (SEND, 0, 0, 11, 3), (SEND, 0, 0, 9, 1), (SEND, 0, 0, 7, 4), (SEND, 0, 0, 3, 2),
    (SEND, 0, 0, 5, 5), (OWN_KEYS,), (TWIN_KEYS,), (TWIN, 0, 0), (NORMALIZE, 1), (TWIN, 0, 1), (NORMALIZE, 2),
    (TWIN, 0, 2), (WAIT_TWIN_KEYS,), (SEND_KEYS, 0, 11, 3), (SEND_KEYS, 0, 9, 1), (SEND_KEYS, 0, 7, 4),
    (SEND_KEYS, 0, 3, 2), (SEND_KEYS, 0, 5, 5), (PREPARE, 0), (WAIT_TWIN, 0), (COMPARE, 0, 0, 2, True, True),
    (FINISH_ROWS, 0), (SEND, 2, 0, 11, 3), (SEND, 1, 0, 9, 1), (SEND, 2, 0, 5, 5), (SEND, 2, 0, 7, 4),
    (SEND, 1, 0, 3, 2), (WAIT, 11, 0), (TWIN, 11, 0), (WAIT_KEYS, 11), (SEND_KEYS, 11, 6, 4), (PREPARE, 11),
    (WAIT, 9, 0), (TWIN, 9, 0), (WAIT_KEYS, 9), (SEND_KEYS, 9, 2, 1), (PREPARE, 9), (WAIT, 7, 0), (WAIT_KEYS, 7),
    (PREPARE, 7), (WAIT, 3, 0), (TWIN, 3, 0), (WAIT_KEYS, 3), (SEND_KEYS, 3, 8, 2), (PREPARE, 3), (WAIT, 5, 0),
    (SEND, 0, 5, 12, 0), (SEND, 1, 0, 11, 3), (SEND, 2, 0, 9, 1), (SEND, 0, 11, 6, 4), (SEND, 1, 0, 5, 5),
    (SEND, 0, 3, 8, 2), (TWIN, 5, 0), (WAIT_KEYS, 5), (SEND_KEYS, 5, 12, 0), (SEND_KEYS, 5, 4, 1), (PREPARE, 5),
    (WAIT, 11, 2), (TWIN, 11, 2), (WAIT, 9, 1), (TWIN, 9, 1), (WAIT, 5, 2), (TWIN, 5, 2), (WAIT, 7, 2), (WAIT, 3, 1),
    (SEND, 2, 5, 12, 0), (SEND, 2, 11, 6, 4), (SEND, 1, 3, 8, 2), (TWIN, 3, 1), (WAIT, 12, 0), (SEND, 1, 9, 2, 1),
    (SEND, 1, 9, 4, 5), (SEND, 2, 11, 8, 3), (TWIN, 12, 0), (WAIT_KEYS, 12), (SEND_KEYS, 12, 10, 0), (PREPARE, 12),
    (WAIT, 6, 0), (TWIN, 6, 0), (WAIT_KEYS, 6), (SEND_KEYS, 6, 1, 3), (PREPARE, 6), (WAIT, 8, 0), (TWIN, 8, 0),
    (WAIT_KEYS, 8), (PREPARE, 8), (WAIT, 11, 1), (TWIN, 11, 1), (WAIT, 9, 2), (TWIN, 9, 2), (WAIT, 5, 1),
    (SEND, 1, 5, 12, 0), (SEND, 1, 11, 6, 4), (SEND, 2, 0, 3, 2), (TWIN, 5, 1), (COMPARE, 9, 0, 0, True, True),
    (FINISH_ROWS, 9), (COMPARE, 11, 0, 0, True, False), (COMPARE, 5, 0, 0, True, False), (SEND, 2, 9, 2, 1),
    (SEND, 2, 9, 4, 5), (SEND, 0, 6, 1, 3), (WAIT_TWIN, 11), (COMPARE, 5, 11, 0, False, True), (WAIT_TWIN, 9),
    (COMPARE, 5, 9, 0, False, True), (FINISH_ROWS, 5), (COMPARE, 11, 9, 0, False, False), (FINISH_ROWS, 11),
    (WAIT, 12, 2), (TWIN, 12, 2), (WAIT, 6, 2), (TWIN, 6, 2), (WAIT, 8, 1), (TWIN, 8, 1), (WAIT, 2, 1), (WAIT, 4, 1),
    (WAIT, 8, 2), (SEND, 2, 12, 10, 0), (SEND, 1, 8, 1, 4), (SEND, 2, 6, 1, 3), (TWIN, 8, 2), (WAIT_TWIN, 5),
    (COMPARE, 8, 5, 0, True, True), (COMPARE, 8, 9, 0, False, False), (FINISH_ROWS, 8),
    (COMPARE, 8, 0, 3, False, False), (SEND, 0, 9, 2, 1), (SEND, 1, 2, 10, 5), (WAIT, 12, 1), (TWIN, 12, 1),
    (WAIT, 6, 1), (TWIN, 6, 1), (WAIT, 3, 2), (TWIN, 3, 2), (WAIT, 1, 0), (SEND, 1, 6, 7, 2), (TWIN, 1, 0),
    (WAIT_KEYS, 1), (PREPARE, 1), (COMPARE, 12, 9, 0, True, False), (COMPARE, 12, 11, 0, False, False),
    (FINISH_COLS, 11, True), (TELL, 11, 0), (TELL, 11, 1), (WAIT_TWIN, 8), (COMPARE, 12, 8, 0, False, True),
    (FINISH_COLS, 8, True), (TELL, 8, 0), (TELL, 8, 1), (FINISH_ROWS, 12), (COMPARE, 6, 5, 0, True, False),
    (WAIT, 2, 2), (WAIT, 4, 2), (SEND, 0, 12, 10, 0), (SEND, 0, 5, 4, 1), (COMPARE, 6, 9, 0, False, False),
    (WAIT_TWIN, 12), (COMPARE, 6, 12, 0, False, True), (FINISH_ROWS, 6), (COMPARE, 3, 12, 0, True, False),
    (COMPARE, 3, 5, 0, False, False), (FINISH_COLS, 5, True), (TELL, 5, 0), (TELL, 5, 1),
    (COMPARE, 3, 9, 0, False, False), (FINISH_ROWS, 3), (WAIT, 10, 2), (TWIN, 10, 2), (WAIT, 1, 1), (TWIN, 1, 1),
    (WAIT, 1, 2), (TWIN, 1, 2), (WAIT, 2, 0), (WAIT_KEYS, 2), (PREPARE, 2), (COMPARE, 1, 12, 0, True, False),
    (COMPARE, 1, 5, 1, False, False), (COMPARE, 1, 9, 0, False, False), (FINISH_ROWS, 1), (FINISH_COLS, 9, True),
    (TELL, 9, 0), (TELL, 9, 1), (COMPARE, 2, 8, 1, True, False), (WAIT, 10, 1), (TWIN, 10, 1), (WAIT_TWIN, 6),
    (COMPARE, 2, 6, 0, False, True), (WAIT_TWIN, 1), (COMPARE, 2, 1, 0, False, True), (FINISH_COLS, 1, True),
    (TELL, 1, 0), (TELL, 1, 1), (WAIT_TWIN, 3), (COMPARE, 2, 3, 0, False, True), (COMPARE, 2, 12, 0, False, False),
    (FINISH_ROWS, 2), (TELL, 2, 0), (WAIT, 10, 0), (TWIN, 10, 0), (WAIT_KEYS, 10), (PREPARE, 10), (WAIT, 7, 1),
    (WAIT, 4, 0), (WAIT_KEYS, 4), (PREPARE, 4), (COMPARE, 10, 3, 0, True, False), (COMPARE, 10, 6, 0, False, False),
    (COMPARE, 10, 1, 1, False, False), (FINISH_ROWS, 10), (TELL, 10, 0), (COMPARE, 7, 12, 0, True, False),
    (FINISH_COLS, 12, True), (TELL, 12, 0), (TELL, 12, 1), (COMPARE, 4, 3, 0, True, False), (FINISH_COLS, 3, True),
    (TELL, 3, 0), (TELL, 3, 1), (COMPARE, 4, 6, 0, False, False), (FINISH_ROWS, 4), (TELL, 4, 0),
    (FINISH_COLS, 6, True), (TELL, 6, 0), (TELL, 6, 1), (COMPARE, 7, 5, 1, False, False), (WAIT_TWIN, 10),
    (COMPARE, 7, 10, 1, False, True), (FINISH_ROWS, 7), (TELL, 7, 0), (COMPARE, 2, 0, 3, False, False),
    (FINISH_COLS, 0, True), (TELL, 0, 1), (DRAIN, 1), (DRAIN, 2), (DRAIN, 3), (DRAIN, 4), (DRAIN, 5), (DRAIN, 6),
    (DRAIN, 7), (DRAIN, 8), (DRAIN, 9), (DRAIN, 10), (DRAIN, 11), (DRAIN, 12), (DRAIN_TWIN, 0), (DRAIN_TWIN, 1),
    (DRAIN_TWIN, 3), (DRAIN_TWIN, 5), (DRAIN_TWIN, 6), (DRAIN_TWIN, 8), (DRAIN_TWIN, 9), (DRAIN_TWIN, 10),
    (DRAIN_TWIN, 11), (DRAIN_TWIN, 12), (DRAIN_TWIN_KEYS,), (HEAR, 11, 0), (HEAR, 11, 1), (HEAR, 8, 0), (HEAR, 8, 1),
    (HEAR, 5, 0), (HEAR, 5, 1), (HEAR, 9, 0), (HEAR, 9, 1), (HEAR, 1, 0), (HEAR, 1, 1), (HEAR, 2, 0), (HEAR, 10, 0),
    (HEAR, 12, 0), (HEAR, 12, 1), (HEAR, 3, 0), (HEAR, 3, 1), (HEAR, 4, 0), (HEAR, 6, 0), (HEAR, 6, 1), (HEAR, 7, 0),
    (HEAR, 0, 1), (DRAIN_TELL, 11, 0), (DRAIN_TELL, 11, 1), (DRAIN_TELL, 8, 0), (DRAIN_TELL, 8, 1),
    (DRAIN_TELL, 5, 0), (DRAIN_TELL, 5, 1), (DRAIN_TELL, 9, 0), (DRAIN_TELL, 9, 1), (DRAIN_TELL, 1, 0),
    (DRAIN_TELL, 1, 1), (DRAIN_TELL, 2, 0), (DRAIN_TELL, 10, 0), (DRAIN_TELL, 12, 0), (DRAIN_TELL, 12, 1),
    (DRAIN_TELL, 3, 0), (DRAIN_TELL, 3, 1), (DRAIN_TELL, 4, 0), (DRAIN_TELL, 6, 0), (DRAIN_TELL, 6, 1),
    (DRAIN_TELL, 7, 0), (DRAIN_TELL, 0, 1),
)
BOTH, ROWS, OWN, COLS = range(4)
STEPS_IN = ((1, 0, 0), (-1, 0, 0), (0, 1, 0), (0, -1, 0), (0, 0, 1), (0, 0, -1))
COUNT = len(STOPS)


def at_offset(offset, other_core):
    z, blk = lax.axis_index("grp"), lax.axis_index("blk")
    core, x, y = blk % 2, blk // 2 % 4, blk // 8
    if other_core:
        core = 1 - core
    x, y, z = (x + offset[0] + 4) % 4, (y + offset[1] + 4) % 4, (z + offset[2] + 4) % 4
    return (z, (y * 4 + x) * 2 + core)


def kernel(
    x_hbm, target_hbm, cluster_hbm, out_ref,
    raw, target, cluster, rows, keys, key_cols, row_max, col_max, parts, heard,
    copied, row_sent, row_got, key_sent, key_got, twin_sent, twin_got, twin_key, part_sent, part_got,
):
    size = raw.shape[0]
    here = (0, 0, 0)
    def piece(part):
        return pl.ds(CUTS[part][0], CUTS[part][1])

    def load(part):
        return pltpu.make_async_copy(x_hbm.at[piece(part)], raw.at[piece(part)], copied.at[part])

    load_target = pltpu.make_async_copy(target_hbm, target, copied.at[CHUNKS])
    load_cluster = pltpu.make_async_copy(cluster_hbm, cluster, copied.at[CHUNKS + 1])
    for part in range(CHUNKS):
        load(part).start()
    load_target.start()
    load_cluster.start()

    barrier = pltpu.get_barrier_semaphore()
    near = [at_offset(step, False) for step in STEPS_IN] + [at_offset(here, True)]
    for device in near:
        pl.semaphore_signal(barrier, inc=1, device_id=device, device_id_type=MESH)

    def normalize(part):
        load(part).wait()
        wide = raw[piece(part)].astype(jnp.float32)
        scale_inv = lax.rsqrt(jnp.sum(wide * wide, axis=1, keepdims=True) + 1e-06)
        rows[0, 0, piece(part)] = (wide * scale_inv).astype(jnp.bfloat16)

    def own_keys():
        load_target.wait()
        load_cluster.wait()
        key = jnp.right_shift(target[...], 5) * 64 + cluster[...]
        keys[0, 0] = key.astype(jnp.float32)

    def remote(src, dst, sent, got, device):
        return pltpu.make_async_remote_copy(
            src_ref=src, dst_ref=dst, send_sem=sent, recv_sem=got, device_id=device, device_id_type=MESH
        )

    def send_rows(part, src, dst, step):
        return remote(
            rows.at[src, 0, piece(part)], rows.at[dst, 0, piece(part)],
            row_sent.at[dst], row_got.at[dst, part], near[step],
        )

    def send_keys(src, dst, step):
        return remote(keys.at[src], keys.at[dst], key_sent.at[dst], key_got.at[dst], near[step])

    def to_twin(slot, where):
        return remote(rows.at[slot, 0, where], rows.at[slot, 1, where], twin_sent.at[slot], twin_got.at[slot], near[6])

    def keys_to_twin():
        return remote(keys.at[0, 0], keys.at[0, 1], twin_key.at[0], twin_key.at[1], near[6])

    def send_part(slot, half):
        offset = tuple(-v for v in STOPS[slot])
        return remote(
            parts.at[slot, half], heard.at[slot, half],
            part_sent.at[slot, half], part_got.at[slot, half], at_offset(offset, half == 1),
        )

    def prepare(slot):
        spread = jnp.broadcast_to(keys[slot, 0], (128, size))
        key_cols[slot] = spread.T

    def compare(left, right, mode, fresh_row, fresh_col):
        best_row = None
        for half in range(2):
            scores = lax.dot_general(
                rows[left, 0], rows[right, half], (((1,), (1,)), ((), ())), preferred_element_type=jnp.float32
            )
            for lane in range(0, size, 128):
                same = key_cols[left] == keys[right, half][:, lane : lane + 128]
                if mode == OWN and half == 0:
                    row_at = lax.broadcasted_iota(jnp.int32, (size, 128), 0)
                    col_at = lax.broadcasted_iota(jnp.int32, (size, 128), 1) + lane
                    same = same & (row_at != col_at)
                block = jnp.where(same, scores[:, lane : lane + 128], LOWEST)
                if mode != COLS:
                    best_row = block if best_row is None else jnp.maximum(best_row, block)
                if mode in (BOTH, COLS):
                    best = jnp.max(block.reshape(size // 8, 8, 128), axis=0)
                    place = (right, half, slice(None), slice(lane, lane + 128))
                    col_max[place] = best if fresh_col else jnp.maximum(col_max[place], best)
        if mode != COLS:
            row_max[left] = best_row if fresh_row else jnp.maximum(row_max[left], best_row)

    def finish_rows(slot):
        parts[slot, 0] = jnp.max(row_max[slot].T, axis=0, keepdims=True)

    def finish_cols(slot, add):
        col = jnp.max(col_max[slot, 0], axis=0, keepdims=True)
        parts[slot, 0] = jnp.maximum(parts[slot, 0], col) if add else col
        parts[slot, 1] = jnp.max(col_max[slot, 1], axis=0, keepdims=True)

    def drain(slot):
        remote(rows.at[0, 0], rows.at[slot, 0], row_sent.at[slot], row_got.at[slot, 0], near[0]).wait_send()
        send_keys(0, slot, 0).wait_send()

    whole = pl.ds(0, size)

    def run(program):
        best = None
        for op, *args in program:
            if op == ENTER:
                pl.semaphore_wait(barrier, len(near))
            elif op == NORMALIZE:
                normalize(*args)
            elif op == OWN_KEYS:
                own_keys()
            elif op == SEND:
                send_rows(*args).start()
            elif op == WAIT:
                send_rows(args[1], 0, args[0], 0).wait_recv()
            elif op == SEND_KEYS:
                send_keys(*args).start()
            elif op == WAIT_KEYS:
                send_keys(0, args[0], 0).wait_recv()
            elif op == TWIN:
                to_twin(args[0], piece(args[1])).start()
            elif op == WAIT_TWIN:
                to_twin(args[0], whole).wait_recv()
            elif op == TWIN_KEYS:
                keys_to_twin().start()
            elif op == WAIT_TWIN_KEYS:
                keys_to_twin().wait_recv()
            elif op == PREPARE:
                prepare(*args)
            elif op == COMPARE:
                compare(*args)
            elif op == FINISH_ROWS:
                finish_rows(*args)
            elif op == FINISH_COLS:
                finish_cols(*args)
            elif op == TELL:
                send_part(*args).start()
            elif op == HEAR:
                send_part(*args).wait_recv()
                news = heard[args[0], args[1]]
                best = news if best is None else jnp.maximum(best, news)
            elif op == DRAIN:
                drain(*args)
            elif op == DRAIN_TWIN:
                to_twin(args[0], whole).wait_send()
            elif op == DRAIN_TWIN_KEYS:
                keys_to_twin().wait_send()
            elif op == DRAIN_TELL:
                send_part(*args).wait_send()
        out_ref[...] = jnp.maximum(best, parts[0, 0])

    run(PROGRAM)


def body(embeddings, target, cluster):
    size, width = embeddings.shape
    hbm, vmem = pl.BlockSpec(memory_space=pltpu.HBM), pl.BlockSpec(memory_space=pltpu.VMEM)
    dma = pltpu.SemaphoreType.DMA
    best = pl.pallas_call(
        kernel,
        out_shape=jax.ShapeDtypeStruct((1, size), jnp.float32),
        in_specs=[hbm] * 3,
        out_specs=vmem,
        scratch_shapes=[
            pltpu.VMEM((size, width), jnp.bfloat16),
            pltpu.VMEM((1, size), jnp.int32),
            pltpu.VMEM((1, size), jnp.int32),
            pltpu.VMEM((COUNT, 2, size, width), jnp.bfloat16),
            pltpu.VMEM((COUNT, 2, 1, size), jnp.float32),
            pltpu.VMEM((COUNT, size, 128), jnp.float32),
            pltpu.VMEM((COUNT, size, 128), jnp.float32),
            pltpu.VMEM((COUNT, 2, 8, size), jnp.float32),
            pltpu.VMEM((COUNT, 2, 1, size), jnp.float32),
            pltpu.VMEM((COUNT, 2, 1, size), jnp.float32),
            dma((CHUNKS + 2,)), dma((COUNT,)), dma((COUNT, CHUNKS)), dma((COUNT,)), dma((COUNT,)),
            dma((COUNT,)), dma((COUNT,)), dma((2,)), dma((COUNT, 2)), dma((COUNT, 2)),
        ],
        compiler_params=pltpu.CompilerParams(
            collective_id=0, has_side_effects=True, vmem_limit_bytes=56553472
        ),
        name="nearest",
    )(embeddings, target.reshape(1, size), cluster.reshape(1, size))
    return best.reshape(size)


def solution(mesh):
    return jax.shard_map(
        body,
        mesh=mesh,
        in_specs=(P(("grp", "blk"), None), P(("grp", "blk"), None), P(("grp", "blk"))),
        out_specs=P(("grp", "blk")),
        check_vma=False,
    )
```

```python
import jax
import jax.numpy as jnp
from jax import lax
from jax.experimental import pallas as pl
from jax.experimental.pallas import tpu as pltpu
from jax.sharding import PartitionSpec as P

MESH = pl.DeviceIdType.MESH
LOWEST = -1.0
CUTS = ((0, 80), (80, 80), (160, 96))
CHUNKS = len(CUTS)
STOPS = (
    (0, 0, 0),
    (1, 0, 0),
    (0, 1, 0),
    (1, 0, 1),
    (-1, 2, 0),
    (-1, -1, 0),
    (0, 2, 0),
    (-1, 0, 0),
    (0, 0, -1),
    (1, 0, 2),
    (0, 0, 2),
    (0, 0, 1),
    (-1, 1, 0),
)
(
    ENTER, NORMALIZE, OWN_KEYS, SEND, WAIT, SEND_KEYS, WAIT_KEYS, TWIN, WAIT_TWIN, TWIN_KEYS, WAIT_TWIN_KEYS, PREPARE, COMPARE, FINISH_ROWS, FINISH_COLS, TELL, HEAR, DRAIN, DRAIN_TWIN, DRAIN_TWIN_KEYS, DRAIN_TELL,
) = range(21)
PROGRAM = (
    (NORMALIZE, 0), (ENTER,), (SEND, 0, 0, 2, 2), (SEND, 0, 0, 11, 4), (SEND, 0, 0, 8, 5), (SEND, 0, 0, 7, 1),
    (SEND, 0, 0, 1, 0), (OWN_KEYS,), (TWIN_KEYS,), (TWIN, 0, 0), (NORMALIZE, 1), (TWIN, 0, 1), (NORMALIZE, 2),
    (TWIN, 0, 2), (WAIT_TWIN_KEYS,), (SEND_KEYS, 0, 2, 2), (SEND_KEYS, 0, 11, 4), (SEND_KEYS, 0, 8, 5),
    (SEND_KEYS, 0, 7, 1), (SEND_KEYS, 0, 1, 0), (PREPARE, 0), (WAIT_TWIN, 0), (COMPARE, 0, 0, 2, True, True),
    (FINISH_ROWS, 0), (SEND, 1, 0, 2, 2), (SEND, 2, 0, 7, 1), (SEND, 1, 0, 11, 4), (SEND, 1, 0, 1, 0),
    (SEND, 2, 0, 8, 5), (WAIT, 2, 0), (TWIN, 2, 0), (WAIT_KEYS, 2), (SEND_KEYS, 2, 6, 2), (PREPARE, 2), (WAIT, 11, 0),
    (TWIN, 11, 0), (WAIT_KEYS, 11), (SEND_KEYS, 11, 3, 0), (PREPARE, 11), (WAIT, 8, 0), (TWIN, 8, 0), (WAIT_KEYS, 8),
    (SEND_KEYS, 8, 10, 5), (PREPARE, 8), (WAIT, 7, 0), (TWIN, 7, 0), (WAIT_KEYS, 7), (SEND_KEYS, 7, 5, 3),
    (PREPARE, 7), (WAIT, 1, 0), (SEND, 0, 7, 5, 3), (SEND, 0, 2, 6, 2), (SEND, 2, 0, 11, 4), (SEND, 0, 11, 3, 0),
    (SEND, 1, 0, 7, 1), (SEND, 1, 0, 8, 5), (TWIN, 1, 0), (WAIT_KEYS, 1), (PREPARE, 1), (WAIT, 2, 1), (TWIN, 2, 1),
    (WAIT, 11, 1), (TWIN, 11, 1), (WAIT, 1, 1), (TWIN, 1, 1), (WAIT, 7, 2), (TWIN, 7, 2), (WAIT, 8, 2),
    (SEND, 2, 7, 5, 3), (SEND, 2, 0, 2, 2), (SEND, 2, 0, 1, 0), (SEND, 1, 2, 12, 1), (SEND, 1, 1, 3, 4),
    (SEND, 2, 8, 10, 5), (TWIN, 8, 2), (WAIT, 5, 0), (TWIN, 5, 0), (WAIT_KEYS, 5), (PREPARE, 5), (WAIT, 6, 0),
    (WAIT_KEYS, 6), (SEND_KEYS, 6, 4, 1), (PREPARE, 6), (WAIT, 3, 0), (TWIN, 3, 0), (WAIT_KEYS, 3),
    (SEND_KEYS, 3, 9, 4), (PREPARE, 3), (WAIT, 11, 2), (TWIN, 11, 2), (WAIT, 7, 1), (TWIN, 7, 1), (WAIT, 8, 1),
    (TWIN, 8, 1), (COMPARE, 7, 0, 0, True, True), (COMPARE, 11, 0, 3, True, False), (SEND, 1, 7, 5, 3),
    (SEND, 0, 3, 9, 4), (SEND, 0, 6, 4, 1), (SEND, 1, 2, 6, 2), (SEND, 2, 11, 3, 0), (COMPARE, 8, 0, 3, True, False),
    (SEND, 0, 8, 10, 5), (WAIT_TWIN, 11), (COMPARE, 8, 11, 1, True, True), (COMPARE, 7, 11, 0, False, True),
    (FINISH_ROWS, 7), (WAIT_TWIN, 7), (COMPARE, 8, 7, 0, False, True), (FINISH_ROWS, 8), (WAIT, 5, 2), (TWIN, 5, 2),
    (WAIT, 2, 2), (TWIN, 2, 2), (WAIT, 1, 2), (TWIN, 1, 2), (WAIT, 12, 1), (WAIT, 3, 1), (TWIN, 3, 1),
    (COMPARE, 1, 7, 1, True, False), (COMPARE, 2, 0, 0, True, False), (WAIT, 10, 2), (SEND, 2, 5, 4, 3),
    (SEND, 1, 12, 4, 2), (SEND, 2, 2, 12, 1), (SEND, 1, 3, 9, 4), (TWIN, 10, 2), (COMPARE, 2, 7, 0, False, False),
    (COMPARE, 2, 11, 0, False, False), (SEND, 2, 10, 9, 0), (SEND, 1, 8, 10, 5), (WAIT_TWIN, 8),
    (COMPARE, 2, 8, 0, False, True), (FINISH_ROWS, 2), (WAIT_TWIN, 2), (COMPARE, 1, 2, 0, False, True),
    (FINISH_ROWS, 1), (WAIT, 5, 1), (TWIN, 5, 1), (WAIT, 9, 0), (WAIT_KEYS, 9), (PREPARE, 9), (WAIT, 4, 0),
    (TWIN, 4, 0), (WAIT_KEYS, 4), (SEND_KEYS, 4, 12, 3), (PREPARE, 4), (WAIT, 6, 1), (COMPARE, 5, 11, 0, True, False),
    (COMPARE, 5, 8, 0, False, False), (WAIT, 3, 2), (TWIN, 3, 2), (WAIT, 10, 0), (SEND, 2, 2, 6, 2), (TWIN, 10, 0),
    (WAIT_KEYS, 10), (PREPARE, 10), (WAIT_TWIN, 1), (COMPARE, 5, 1, 0, False, True), (FINISH_COLS, 1, True),
    (TELL, 1, 0), (TELL, 1, 1), (COMPARE, 5, 2, 0, False, False), (FINISH_ROWS, 5), (SEND, 0, 4, 12, 3),
    (COMPARE, 3, 7, 0, True, False), (FINISH_COLS, 7, True), (TELL, 7, 0), (TELL, 7, 1),
    (COMPARE, 3, 8, 0, False, False), (COMPARE, 3, 2, 0, False, False), (WAIT_TWIN, 5),
    (COMPARE, 3, 5, 0, False, True), (FINISH_ROWS, 3), (WAIT, 4, 1), (TWIN, 4, 1), (WAIT, 9, 1), (WAIT, 4, 2),
    (TWIN, 4, 2), (WAIT, 12, 2), (WAIT, 10, 1), (TWIN, 10, 1), (COMPARE, 4, 11, 0, True, False), (WAIT_TWIN, 3),
    (COMPARE, 4, 3, 0, False, True), (WAIT, 9, 2), (COMPARE, 4, 8, 0, False, False), (COMPARE, 4, 1, 1, False, False),
    (FINISH_ROWS, 4), (COMPARE, 9, 5, 0, True, False), (COMPARE, 9, 2, 0, False, False),
    (COMPARE, 9, 7, 1, False, False), (WAIT_TWIN, 4), (COMPARE, 10, 4, 0, True, True), (FINISH_COLS, 4, True),
    (TELL, 4, 0), (TELL, 4, 1), (COMPARE, 9, 4, 1, False, False), (FINISH_ROWS, 9), (TELL, 9, 0),
    (COMPARE, 10, 5, 0, False, False), (FINISH_COLS, 5, True), (TELL, 5, 0), (TELL, 5, 1),
    (COMPARE, 10, 2, 0, False, False), (FINISH_COLS, 2, True), (TELL, 2, 0), (TELL, 2, 1), (FINISH_ROWS, 10),
    (TELL, 10, 0), (WAIT, 12, 0), (WAIT_KEYS, 12), (PREPARE, 12), (WAIT, 6, 2), (COMPARE, 12, 3, 0, True, False),
    (FINISH_COLS, 3, True), (TELL, 3, 0), (TELL, 3, 1), (COMPARE, 12, 8, 0, False, False), (FINISH_COLS, 8, True),
    (TELL, 8, 0), (TELL, 8, 1), (FINISH_ROWS, 12), (TELL, 12, 0), (COMPARE, 6, 11, 0, True, False),
    (FINISH_COLS, 11, False), (TELL, 11, 0), (TELL, 11, 1), (WAIT_TWIN, 10), (COMPARE, 6, 10, 1, False, True),
    (FINISH_ROWS, 6), (TELL, 6, 0), (COMPARE, 6, 0, 3, False, False), (FINISH_COLS, 0, True), (TELL, 0, 1),
    (DRAIN, 1), (DRAIN, 2), (DRAIN, 3), (DRAIN, 4), (DRAIN, 5), (DRAIN, 6), (DRAIN, 7), (DRAIN, 8), (DRAIN, 9),
    (DRAIN, 10), (DRAIN, 11), (DRAIN, 12), (DRAIN_TWIN, 0), (DRAIN_TWIN, 1), (DRAIN_TWIN, 2), (DRAIN_TWIN, 3),
    (DRAIN_TWIN, 4), (DRAIN_TWIN, 5), (DRAIN_TWIN, 7), (DRAIN_TWIN, 8), (DRAIN_TWIN, 10), (DRAIN_TWIN, 11),
    (DRAIN_TWIN_KEYS,), (HEAR, 1, 0), (HEAR, 1, 1), (HEAR, 7, 0), (HEAR, 7, 1), (HEAR, 4, 0), (HEAR, 4, 1),
    (HEAR, 9, 0), (HEAR, 5, 0), (HEAR, 5, 1), (HEAR, 2, 0), (HEAR, 2, 1), (HEAR, 10, 0), (HEAR, 3, 0), (HEAR, 3, 1),
    (HEAR, 8, 0), (HEAR, 8, 1), (HEAR, 12, 0), (HEAR, 11, 0), (HEAR, 11, 1), (HEAR, 6, 0), (HEAR, 0, 1),
    (DRAIN_TELL, 1, 0), (DRAIN_TELL, 1, 1), (DRAIN_TELL, 7, 0), (DRAIN_TELL, 7, 1), (DRAIN_TELL, 4, 0),
    (DRAIN_TELL, 4, 1), (DRAIN_TELL, 9, 0), (DRAIN_TELL, 5, 0), (DRAIN_TELL, 5, 1), (DRAIN_TELL, 2, 0),
    (DRAIN_TELL, 2, 1), (DRAIN_TELL, 10, 0), (DRAIN_TELL, 3, 0), (DRAIN_TELL, 3, 1), (DRAIN_TELL, 8, 0),
    (DRAIN_TELL, 8, 1), (DRAIN_TELL, 12, 0), (DRAIN_TELL, 11, 0), (DRAIN_TELL, 11, 1), (DRAIN_TELL, 6, 0),
    (DRAIN_TELL, 0, 1),
)
BOTH, ROWS, OWN, COLS = range(4)
STEPS_IN = ((1, 0, 0), (-1, 0, 0), (0, 1, 0), (0, -1, 0), (0, 0, 1), (0, 0, -1))
COUNT = len(STOPS)


def at_offset(offset, other_core):
    z, blk = lax.axis_index("grp"), lax.axis_index("blk")
    core, x, y = blk % 2, blk // 2 % 4, blk // 8
    if other_core:
        core = 1 - core
    x, y, z = (x + offset[0] + 4) % 4, (y + offset[1] + 4) % 4, (z + offset[2] + 4) % 4
    return (z, (y * 4 + x) * 2 + core)


def kernel(
    x_hbm, target_hbm, cluster_hbm, out_ref,
    raw, target, cluster, rows, keys, key_cols, row_max, col_max, parts, heard,
    copied, row_sent, row_got, key_sent, key_got, twin_sent, twin_got, twin_key, part_sent, part_got,
):
    size = raw.shape[0]
    here = (0, 0, 0)
    def piece(part):
        return pl.ds(CUTS[part][0], CUTS[part][1])

    def load(part):
        return pltpu.make_async_copy(x_hbm.at[piece(part)], raw.at[piece(part)], copied.at[part])

    load_target = pltpu.make_async_copy(target_hbm, target, copied.at[CHUNKS])
    load_cluster = pltpu.make_async_copy(cluster_hbm, cluster, copied.at[CHUNKS + 1])
    for part in range(CHUNKS):
        load(part).start()
    load_target.start()
    load_cluster.start()

    barrier = pltpu.get_barrier_semaphore()
    near = [at_offset(step, False) for step in STEPS_IN] + [at_offset(here, True)]
    for device in near:
        pl.semaphore_signal(barrier, inc=1, device_id=device, device_id_type=MESH)

    def normalize(part):
        load(part).wait()
        wide = raw[piece(part)].astype(jnp.float32)
        scale_inv = lax.rsqrt(jnp.sum(wide * wide, axis=1, keepdims=True) + 1e-06)
        rows[0, 0, piece(part)] = (wide * scale_inv).astype(jnp.bfloat16)

    def own_keys():
        load_target.wait()
        load_cluster.wait()
        key = jnp.right_shift(target[...], 5) * 64 + cluster[...]
        keys[0, 0] = key.astype(jnp.float32)

    def remote(src, dst, sent, got, device):
        return pltpu.make_async_remote_copy(
            src_ref=src, dst_ref=dst, send_sem=sent, recv_sem=got, device_id=device, device_id_type=MESH
        )

    def send_rows(part, src, dst, step):
        return remote(
            rows.at[src, 0, piece(part)], rows.at[dst, 0, piece(part)],
            row_sent.at[dst], row_got.at[dst, part], near[step],
        )

    def send_keys(src, dst, step):
        return remote(keys.at[src], keys.at[dst], key_sent.at[dst], key_got.at[dst], near[step])

    def to_twin(slot, where):
        return remote(rows.at[slot, 0, where], rows.at[slot, 1, where], twin_sent.at[slot], twin_got.at[slot], near[6])

    def keys_to_twin():
        return remote(keys.at[0, 0], keys.at[0, 1], twin_key.at[0], twin_key.at[1], near[6])

    def send_part(slot, half):
        offset = tuple(-v for v in STOPS[slot])
        return remote(
            parts.at[slot, half], heard.at[slot, half],
            part_sent.at[slot, half], part_got.at[slot, half], at_offset(offset, half == 1),
        )

    def prepare(slot):
        spread = jnp.broadcast_to(keys[slot, 0], (128, size))
        key_cols[slot] = spread.T

    def compare(left, right, mode, fresh_row, fresh_col):
        best_row = None
        for half in range(2):
            scores = lax.dot_general(
                rows[left, 0], rows[right, half], (((1,), (1,)), ((), ())), preferred_element_type=jnp.float32
            )
            for lane in range(0, size, 128):
                same = key_cols[left] == keys[right, half][:, lane : lane + 128]
                if mode == OWN and half == 0:
                    row_at = lax.broadcasted_iota(jnp.int32, (size, 128), 0)
                    col_at = lax.broadcasted_iota(jnp.int32, (size, 128), 1) + lane
                    same = same & (row_at != col_at)
                block = jnp.where(same, scores[:, lane : lane + 128], LOWEST)
                if mode != COLS:
                    best_row = block if best_row is None else jnp.maximum(best_row, block)
                if mode in (BOTH, COLS):
                    best = jnp.max(block.reshape(size // 8, 8, 128), axis=0)
                    place = (right, half, slice(None), slice(lane, lane + 128))
                    col_max[place] = best if fresh_col else jnp.maximum(col_max[place], best)
        if mode != COLS:
            row_max[left] = best_row if fresh_row else jnp.maximum(row_max[left], best_row)

    def finish_rows(slot):
        parts[slot, 0] = jnp.max(row_max[slot].T, axis=0, keepdims=True)

    def finish_cols(slot, add):
        col = jnp.max(col_max[slot, 0], axis=0, keepdims=True)
        parts[slot, 0] = jnp.maximum(parts[slot, 0], col) if add else col
        parts[slot, 1] = jnp.max(col_max[slot, 1], axis=0, keepdims=True)

    def drain(slot):
        remote(rows.at[0, 0], rows.at[slot, 0], row_sent.at[slot], row_got.at[slot, 0], near[0]).wait_send()
        send_keys(0, slot, 0).wait_send()

    whole = pl.ds(0, size)

    def run(program):
        best = None
        for op, *args in program:
            if op == ENTER:
                pl.semaphore_wait(barrier, len(near))
            elif op == NORMALIZE:
                normalize(*args)
            elif op == OWN_KEYS:
                own_keys()
            elif op == SEND:
                send_rows(*args).start()
            elif op == WAIT:
                send_rows(args[1], 0, args[0], 0).wait_recv()
            elif op == SEND_KEYS:
                send_keys(*args).start()
            elif op == WAIT_KEYS:
                send_keys(0, args[0], 0).wait_recv()
            elif op == TWIN:
                to_twin(args[0], piece(args[1])).start()
            elif op == WAIT_TWIN:
                to_twin(args[0], whole).wait_recv()
            elif op == TWIN_KEYS:
                keys_to_twin().start()
            elif op == WAIT_TWIN_KEYS:
                keys_to_twin().wait_recv()
            elif op == PREPARE:
                prepare(*args)
            elif op == COMPARE:
                compare(*args)
            elif op == FINISH_ROWS:
                finish_rows(*args)
            elif op == FINISH_COLS:
                finish_cols(*args)
            elif op == TELL:
                send_part(*args).start()
            elif op == HEAR:
                send_part(*args).wait_recv()
                news = heard[args[0], args[1]]
                best = news if best is None else jnp.maximum(best, news)
            elif op == DRAIN:
                drain(*args)
            elif op == DRAIN_TWIN:
                to_twin(args[0], whole).wait_send()
            elif op == DRAIN_TWIN_KEYS:
                keys_to_twin().wait_send()
            elif op == DRAIN_TELL:
                send_part(*args).wait_send()
        out_ref[...] = jnp.maximum(best, parts[0, 0])

    run(PROGRAM)


def body(embeddings, target, cluster):
    size, width = embeddings.shape
    hbm, vmem = pl.BlockSpec(memory_space=pltpu.HBM), pl.BlockSpec(memory_space=pltpu.VMEM)
    dma = pltpu.SemaphoreType.DMA
    best = pl.pallas_call(
        kernel,
        out_shape=jax.ShapeDtypeStruct((1, size), jnp.float32),
        in_specs=[hbm] * 3,
        out_specs=vmem,
        scratch_shapes=[
            pltpu.VMEM((size, width), jnp.bfloat16),
            pltpu.VMEM((1, size), jnp.int32),
            pltpu.VMEM((1, size), jnp.int32),
            pltpu.VMEM((COUNT, 2, size, width), jnp.bfloat16),
            pltpu.VMEM((COUNT, 2, 1, size), jnp.float32),
            pltpu.VMEM((COUNT, size, 128), jnp.float32),
            pltpu.VMEM((COUNT, size, 128), jnp.float32),
            pltpu.VMEM((COUNT, 2, 8, size), jnp.float32),
            pltpu.VMEM((COUNT, 2, 1, size), jnp.float32),
            pltpu.VMEM((COUNT, 2, 1, size), jnp.float32),
            dma((CHUNKS + 2,)), dma((COUNT,)), dma((COUNT, CHUNKS)), dma((COUNT,)), dma((COUNT,)),
            dma((COUNT,)), dma((COUNT,)), dma((2,)), dma((COUNT, 2)), dma((COUNT, 2)),
        ],
        compiler_params=pltpu.CompilerParams(
            collective_id=0, has_side_effects=True, vmem_limit_bytes=56553472
        ),
        name="nearest",
    )(embeddings, target.reshape(1, size), cluster.reshape(1, size))
    return best.reshape(size)


def solution(mesh):
    return jax.shard_map(
        body,
        mesh=mesh,
        in_specs=(P(("grp", "blk"), None), P(("grp", "blk"), None), P(("grp", "blk"))),
        out_specs=P(("grp", "blk")),
        check_vma=False,
    )
```

```python
import jax
import jax.numpy as jnp
from jax import lax
from jax.experimental import pallas as pl
from jax.experimental.pallas import tpu as pltpu
from jax.sharding import PartitionSpec as P

MESH = pl.DeviceIdType.MESH
LOWEST = -1.0
CUTS = ((0, 80), (80, 80), (160, 96))
CHUNKS = len(CUTS)
STOPS = (
    (0, 0, 0),
    (1, 0, 0),
    (0, 1, 0),
    (1, 0, 1),
    (-1, 2, 0),
    (-1, -1, 0),
    (0, 2, 0),
    (-1, 0, 0),
    (0, 0, -1),
    (1, 0, 2),
    (0, 0, 2),
    (0, 0, 1),
    (-1, 1, 0),
)
(
    ENTER, NORMALIZE, OWN_KEYS, SEND, WAIT, SEND_KEYS, WAIT_KEYS, TWIN, WAIT_TWIN, TWIN_KEYS, WAIT_TWIN_KEYS, PREPARE, COMPARE, FINISH_ROWS, FINISH_COLS, TELL, HEAR, DRAIN, DRAIN_TWIN, DRAIN_TWIN_KEYS, DRAIN_TELL,
) = range(21)
PROGRAM = (
    (NORMALIZE, 0), (ENTER,), (SEND, 0, 0, 2, 2), (SEND, 0, 0, 11, 4), (SEND, 0, 0, 8, 5), (SEND, 0, 0, 7, 1),
    (SEND, 0, 0, 1, 0), (OWN_KEYS,), (TWIN_KEYS,), (TWIN, 0, 0), (NORMALIZE, 1), (TWIN, 0, 1), (NORMALIZE, 2),
    (TWIN, 0, 2), (WAIT_TWIN_KEYS,), (SEND_KEYS, 0, 2, 2), (SEND_KEYS, 0, 11, 4), (SEND_KEYS, 0, 8, 5),
    (SEND_KEYS, 0, 7, 1), (SEND_KEYS, 0, 1, 0), (PREPARE, 0), (WAIT_TWIN, 0), (COMPARE, 0, 0, 2, True, True),
    (FINISH_ROWS, 0), (SEND, 1, 0, 2, 2), (SEND, 2, 0, 7, 1), (SEND, 1, 0, 11, 4), (SEND, 1, 0, 1, 0),
    (SEND, 2, 0, 8, 5), (WAIT, 2, 0), (TWIN, 2, 0), (WAIT_KEYS, 2), (SEND_KEYS, 2, 6, 2), (PREPARE, 2), (WAIT, 11, 0),
    (TWIN, 11, 0), (WAIT_KEYS, 11), (SEND_KEYS, 11, 3, 0), (PREPARE, 11), (WAIT, 8, 0), (TWIN, 8, 0), (WAIT_KEYS, 8),
    (SEND_KEYS, 8, 10, 5), (PREPARE, 8), (WAIT, 7, 0), (TWIN, 7, 0), (WAIT_KEYS, 7), (SEND_KEYS, 7, 5, 3),
    (PREPARE, 7), (WAIT, 1, 0), (SEND, 0, 7, 5, 3), (SEND, 0, 2, 6, 2), (SEND, 2, 0, 11, 4), (SEND, 0, 11, 3, 0),
    (SEND, 1, 0, 7, 1), (SEND, 1, 0, 8, 5), (TWIN, 1, 0), (WAIT_KEYS, 1), (PREPARE, 1), (WAIT, 2, 1), (TWIN, 2, 1),
    (WAIT, 11, 1), (TWIN, 11, 1), (WAIT, 1, 1), (TWIN, 1, 1), (WAIT, 7, 2), (TWIN, 7, 2), (WAIT, 8, 2),
    (SEND, 2, 7, 5, 3), (SEND, 2, 0, 2, 2), (SEND, 2, 0, 1, 0), (SEND, 1, 2, 12, 1), (SEND, 1, 1, 3, 4),
    (SEND, 2, 8, 10, 5), (TWIN, 8, 2), (WAIT, 5, 0), (TWIN, 5, 0), (WAIT_KEYS, 5), (PREPARE, 5), (WAIT, 6, 0),
    (WAIT_KEYS, 6), (SEND_KEYS, 6, 4, 1), (PREPARE, 6), (WAIT, 3, 0), (TWIN, 3, 0), (WAIT_KEYS, 3),
    (SEND_KEYS, 3, 9, 4), (PREPARE, 3), (WAIT, 11, 2), (TWIN, 11, 2), (WAIT, 7, 1), (TWIN, 7, 1), (WAIT, 8, 1),
    (TWIN, 8, 1), (COMPARE, 7, 0, 0, True, True), (COMPARE, 11, 0, 3, True, False), (SEND, 1, 7, 5, 3),
    (SEND, 0, 3, 9, 4), (SEND, 0, 6, 4, 1), (SEND, 1, 2, 6, 2), (SEND, 2, 11, 3, 0), (COMPARE, 8, 0, 3, True, False),
    (SEND, 0, 8, 10, 5), (WAIT_TWIN, 11), (COMPARE, 8, 11, 1, True, True), (COMPARE, 7, 11, 0, False, True),
    (FINISH_ROWS, 7), (WAIT_TWIN, 7), (COMPARE, 8, 7, 0, False, True), (FINISH_ROWS, 8), (WAIT, 5, 2), (TWIN, 5, 2),
    (WAIT, 2, 2), (TWIN, 2, 2), (WAIT, 1, 2), (TWIN, 1, 2), (WAIT, 12, 1), (WAIT, 3, 1), (TWIN, 3, 1),
    (COMPARE, 1, 7, 1, True, False), (COMPARE, 2, 0, 0, True, False), (WAIT, 10, 2), (SEND, 2, 5, 4, 3),
    (SEND, 1, 12, 4, 2), (SEND, 2, 2, 12, 1), (SEND, 1, 3, 9, 4), (TWIN, 10, 2), (COMPARE, 2, 7, 0, False, False),
    (COMPARE, 2, 11, 0, False, False), (SEND, 2, 10, 9, 0), (SEND, 1, 8, 10, 5), (WAIT_TWIN, 8),
    (COMPARE, 2, 8, 0, False, True), (FINISH_ROWS, 2), (WAIT_TWIN, 2), (COMPARE, 1, 2, 0, False, True),
    (FINISH_ROWS, 1), (WAIT, 5, 1), (TWIN, 5, 1), (WAIT, 9, 0), (WAIT_KEYS, 9), (PREPARE, 9), (WAIT, 4, 0),
    (TWIN, 4, 0), (WAIT_KEYS, 4), (SEND_KEYS, 4, 12, 3), (PREPARE, 4), (WAIT, 6, 1), (COMPARE, 5, 11, 0, True, False),
    (COMPARE, 5, 8, 0, False, False), (WAIT, 3, 2), (TWIN, 3, 2), (WAIT, 10, 0), (SEND, 2, 2, 6, 2), (TWIN, 10, 0),
    (WAIT_KEYS, 10), (PREPARE, 10), (WAIT_TWIN, 1), (COMPARE, 5, 1, 0, False, True), (FINISH_COLS, 1, True),
    (TELL, 1, 0), (TELL, 1, 1), (COMPARE, 5, 2, 0, False, False), (FINISH_ROWS, 5), (SEND, 0, 4, 12, 3),
    (COMPARE, 3, 7, 0, True, False), (FINISH_COLS, 7, True), (TELL, 7, 0), (TELL, 7, 1),
    (COMPARE, 3, 8, 0, False, False), (COMPARE, 3, 2, 0, False, False), (WAIT_TWIN, 5),
    (COMPARE, 3, 5, 0, False, True), (FINISH_ROWS, 3), (WAIT, 4, 1), (TWIN, 4, 1), (WAIT, 9, 1), (WAIT, 4, 2),
    (TWIN, 4, 2), (WAIT, 12, 2), (WAIT, 10, 1), (TWIN, 10, 1), (COMPARE, 4, 11, 0, True, False), (WAIT_TWIN, 3),
    (COMPARE, 4, 3, 0, False, True), (WAIT, 9, 2), (COMPARE, 4, 8, 0, False, False), (COMPARE, 4, 1, 1, False, False),
    (FINISH_ROWS, 4), (COMPARE, 9, 5, 0, True, False), (COMPARE, 9, 2, 0, False, False),
    (COMPARE, 9, 7, 1, False, False), (WAIT_TWIN, 4), (COMPARE, 10, 4, 0, True, True), (FINISH_COLS, 4, True),
    (TELL, 4, 0), (TELL, 4, 1), (COMPARE, 9, 4, 1, False, False), (FINISH_ROWS, 9), (TELL, 9, 0),
    (COMPARE, 10, 5, 0, False, False), (FINISH_COLS, 5, True), (TELL, 5, 0), (TELL, 5, 1),
    (COMPARE, 10, 2, 0, False, False), (FINISH_COLS, 2, True), (TELL, 2, 0), (TELL, 2, 1), (FINISH_ROWS, 10),
    (TELL, 10, 0), (WAIT, 12, 0), (WAIT_KEYS, 12), (PREPARE, 12), (WAIT, 6, 2), (COMPARE, 12, 3, 0, True, False),
    (FINISH_COLS, 3, True), (TELL, 3, 0), (TELL, 3, 1), (COMPARE, 12, 8, 0, False, False), (FINISH_COLS, 8, True),
    (TELL, 8, 0), (TELL, 8, 1), (FINISH_ROWS, 12), (TELL, 12, 0), (COMPARE, 6, 11, 0, True, False),
    (FINISH_COLS, 11, False), (TELL, 11, 0), (TELL, 11, 1), (WAIT_TWIN, 10), (COMPARE, 6, 10, 1, False, True),
    (FINISH_ROWS, 6), (TELL, 6, 0), (COMPARE, 6, 0, 3, False, False), (FINISH_COLS, 0, True), (TELL, 0, 1),
    (DRAIN, 1), (DRAIN, 2), (DRAIN, 3), (DRAIN, 4), (DRAIN, 5), (DRAIN, 6), (DRAIN, 7), (DRAIN, 8), (DRAIN, 9),
    (DRAIN, 10), (DRAIN, 11), (DRAIN, 12), (DRAIN_TWIN, 0), (DRAIN_TWIN, 1), (DRAIN_TWIN, 2), (DRAIN_TWIN, 3),
    (DRAIN_TWIN, 4), (DRAIN_TWIN, 5), (DRAIN_TWIN, 7), (DRAIN_TWIN, 8), (DRAIN_TWIN, 10), (DRAIN_TWIN, 11),
    (DRAIN_TWIN_KEYS,), (HEAR, 1, 0), (HEAR, 1, 1), (HEAR, 7, 0), (HEAR, 7, 1), (HEAR, 4, 0), (HEAR, 4, 1),
    (HEAR, 9, 0), (HEAR, 5, 0), (HEAR, 5, 1), (HEAR, 2, 0), (HEAR, 2, 1), (HEAR, 10, 0), (HEAR, 3, 0), (HEAR, 3, 1),
    (HEAR, 8, 0), (HEAR, 8, 1), (HEAR, 12, 0), (HEAR, 11, 0), (HEAR, 11, 1), (HEAR, 6, 0), (HEAR, 0, 1),
    (DRAIN_TELL, 1, 0), (DRAIN_TELL, 1, 1), (DRAIN_TELL, 7, 0), (DRAIN_TELL, 7, 1), (DRAIN_TELL, 4, 0),
    (DRAIN_TELL, 4, 1), (DRAIN_TELL, 9, 0), (DRAIN_TELL, 5, 0), (DRAIN_TELL, 5, 1), (DRAIN_TELL, 2, 0),
    (DRAIN_TELL, 2, 1), (DRAIN_TELL, 10, 0), (DRAIN_TELL, 3, 0), (DRAIN_TELL, 3, 1), (DRAIN_TELL, 8, 0),
    (DRAIN_TELL, 8, 1), (DRAIN_TELL, 12, 0), (DRAIN_TELL, 11, 0), (DRAIN_TELL, 11, 1), (DRAIN_TELL, 6, 0),
    (DRAIN_TELL, 0, 1),
)
BOTH, ROWS, OWN, COLS = range(4)
STEPS_IN = ((1, 0, 0), (-1, 0, 0), (0, 1, 0), (0, -1, 0), (0, 0, 1), (0, 0, -1))
COUNT = len(STOPS)


def at_offset(offset, other_core):
    z, blk = lax.axis_index("grp"), lax.axis_index("blk")
    core, x, y = blk % 2, blk // 2 % 4, blk // 8
    if other_core:
        core = 1 - core
    x, y, z = (x + offset[0] + 4) % 4, (y + offset[1] + 4) % 4, (z + offset[2] + 4) % 4
    return (z, (y * 4 + x) * 2 + core)


def kernel(
    x_hbm, target_hbm, cluster_hbm, out_ref,
    raw, target, cluster, rows, keys, key_cols, row_max, col_max, parts, heard,
    copied, row_sent, row_got, key_sent, key_got, twin_sent, twin_got, twin_key, part_sent, part_got,
):
    size = raw.shape[0]
    here = (0, 0, 0)
    barrier = pltpu.get_barrier_semaphore()
    near = [at_offset(step, False) for step in STEPS_IN] + [at_offset(here, True)]
    for device in near:
        pl.semaphore_signal(barrier, inc=1, device_id=device, device_id_type=MESH)

    def piece(part):
        return pl.ds(CUTS[part][0], CUTS[part][1])

    def load(part):
        return pltpu.make_async_copy(x_hbm.at[piece(part)], raw.at[piece(part)], copied.at[part])

    load_target = pltpu.make_async_copy(target_hbm, target, copied.at[CHUNKS])
    load_cluster = pltpu.make_async_copy(cluster_hbm, cluster, copied.at[CHUNKS + 1])
    for part in range(CHUNKS):
        load(part).start()
    load_target.start()
    load_cluster.start()

    def normalize(part):
        load(part).wait()
        wide = raw[piece(part)].astype(jnp.float32)
        scale_inv = lax.rsqrt(jnp.sum(wide * wide, axis=1, keepdims=True) + 1e-06)
        rows[0, 0, piece(part)] = (wide * scale_inv).astype(jnp.bfloat16)

    def own_keys():
        load_target.wait()
        load_cluster.wait()
        key = jnp.right_shift(target[...], 5) * 64 + cluster[...]
        keys[0, 0] = key.astype(jnp.float32)

    def remote(src, dst, sent, got, device):
        return pltpu.make_async_remote_copy(
            src_ref=src, dst_ref=dst, send_sem=sent, recv_sem=got, device_id=device, device_id_type=MESH
        )

    def send_rows(part, src, dst, step):
        return remote(
            rows.at[src, 0, piece(part)], rows.at[dst, 0, piece(part)],
            row_sent.at[dst], row_got.at[dst, part], near[step],
        )

    def send_keys(src, dst, step):
        return remote(keys.at[src], keys.at[dst], key_sent.at[dst], key_got.at[dst], near[step])

    def to_twin(slot, where):
        return remote(rows.at[slot, 0, where], rows.at[slot, 1, where], twin_sent.at[slot], twin_got.at[slot], near[6])

    def keys_to_twin():
        return remote(keys.at[0, 0], keys.at[0, 1], twin_key.at[0], twin_key.at[1], near[6])

    def send_part(slot, half):
        offset = tuple(-v for v in STOPS[slot])
        return remote(
            parts.at[slot, half], heard.at[slot, half],
            part_sent.at[slot, half], part_got.at[slot, half], at_offset(offset, half == 1),
        )

    def prepare(slot):
        spread = jnp.broadcast_to(keys[slot, 0], (128, size))
        key_cols[slot] = spread.T

    def compare(left, right, mode, fresh_row, fresh_col):
        best_row = None
        for half in range(2):
            scores = lax.dot_general(
                rows[left, 0], rows[right, half], (((1,), (1,)), ((), ())), preferred_element_type=jnp.float32
            )
            for lane in range(0, size, 128):
                same = key_cols[left] == keys[right, half][:, lane : lane + 128]
                if mode == OWN and half == 0:
                    row_at = lax.broadcasted_iota(jnp.int32, (size, 128), 0)
                    col_at = lax.broadcasted_iota(jnp.int32, (size, 128), 1) + lane
                    same = same & (row_at != col_at)
                block = jnp.where(same, scores[:, lane : lane + 128], LOWEST)
                if mode != COLS:
                    best_row = block if best_row is None else jnp.maximum(best_row, block)
                if mode in (BOTH, COLS):
                    best = jnp.max(block.reshape(size // 8, 8, 128), axis=0)
                    place = (right, half, slice(None), slice(lane, lane + 128))
                    col_max[place] = best if fresh_col else jnp.maximum(col_max[place], best)
        if mode != COLS:
            row_max[left] = best_row if fresh_row else jnp.maximum(row_max[left], best_row)

    def finish_rows(slot):
        parts[slot, 0] = jnp.max(row_max[slot].T, axis=0, keepdims=True)

    def finish_cols(slot, add):
        col = jnp.max(col_max[slot, 0], axis=0, keepdims=True)
        parts[slot, 0] = jnp.maximum(parts[slot, 0], col) if add else col
        parts[slot, 1] = jnp.max(col_max[slot, 1], axis=0, keepdims=True)

    def drain(slot):
        remote(rows.at[0, 0], rows.at[slot, 0], row_sent.at[slot], row_got.at[slot, 0], near[0]).wait_send()
        send_keys(0, slot, 0).wait_send()

    whole = pl.ds(0, size)

    def run(program):
        best = None
        for op, *args in program:
            if op == ENTER:
                pl.semaphore_wait(barrier, len(near))
            elif op == NORMALIZE:
                normalize(*args)
            elif op == OWN_KEYS:
                own_keys()
            elif op == SEND:
                send_rows(*args).start()
            elif op == WAIT:
                send_rows(args[1], 0, args[0], 0).wait_recv()
            elif op == SEND_KEYS:
                send_keys(*args).start()
            elif op == WAIT_KEYS:
                send_keys(0, args[0], 0).wait_recv()
            elif op == TWIN:
                to_twin(args[0], piece(args[1])).start()
            elif op == WAIT_TWIN:
                to_twin(args[0], whole).wait_recv()
            elif op == TWIN_KEYS:
                keys_to_twin().start()
            elif op == WAIT_TWIN_KEYS:
                keys_to_twin().wait_recv()
            elif op == PREPARE:
                prepare(*args)
            elif op == COMPARE:
                compare(*args)
            elif op == FINISH_ROWS:
                finish_rows(*args)
            elif op == FINISH_COLS:
                finish_cols(*args)
            elif op == TELL:
                send_part(*args).start()
            elif op == HEAR:
                send_part(*args).wait_recv()
                news = heard[args[0], args[1]]
                best = news if best is None else jnp.maximum(best, news)
            elif op == DRAIN:
                drain(*args)
            elif op == DRAIN_TWIN:
                to_twin(args[0], whole).wait_send()
            elif op == DRAIN_TWIN_KEYS:
                keys_to_twin().wait_send()
            elif op == DRAIN_TELL:
                send_part(*args).wait_send()
        out_ref[...] = jnp.maximum(best, parts[0, 0])

    run(PROGRAM)


def body(embeddings, target, cluster):
    size, width = embeddings.shape
    hbm, vmem = pl.BlockSpec(memory_space=pltpu.HBM), pl.BlockSpec(memory_space=pltpu.VMEM)
    dma = pltpu.SemaphoreType.DMA
    best = pl.pallas_call(
        kernel,
        out_shape=jax.ShapeDtypeStruct((1, size), jnp.float32),
        in_specs=[hbm] * 3,
        out_specs=vmem,
        scratch_shapes=[
            pltpu.VMEM((size, width), jnp.bfloat16),
            pltpu.VMEM((1, size), jnp.int32),
            pltpu.VMEM((1, size), jnp.int32),
            pltpu.VMEM((COUNT, 2, size, width), jnp.bfloat16),
            pltpu.VMEM((COUNT, 2, 1, size), jnp.float32),
            pltpu.VMEM((COUNT, size, 128), jnp.float32),
            pltpu.VMEM((COUNT, size, 128), jnp.float32),
            pltpu.VMEM((COUNT, 2, 8, size), jnp.float32),
            pltpu.VMEM((COUNT, 2, 1, size), jnp.float32),
            pltpu.VMEM((COUNT, 2, 1, size), jnp.float32),
            dma((CHUNKS + 2,)), dma((COUNT,)), dma((COUNT, CHUNKS)), dma((COUNT,)), dma((COUNT,)),
            dma((COUNT,)), dma((COUNT,)), dma((2,)), dma((COUNT, 2)), dma((COUNT, 2)),
        ],
        compiler_params=pltpu.CompilerParams(
            collective_id=0, has_side_effects=True, vmem_limit_bytes=56553472
        ),
        name="nearest",
    )(embeddings, target.reshape(1, size), cluster.reshape(1, size))
    return best.reshape(size)


def solution(mesh):
    return jax.shard_map(
        body,
        mesh=mesh,
        in_specs=(P(("grp", "blk"), None), P(("grp", "blk"), None), P(("grp", "blk"))),
        out_specs=P(("grp", "blk")),
        check_vma=False,
    )
```

```python
import jax
import jax.numpy as jnp
from jax import lax
from jax.experimental import pallas as pl
from jax.experimental.pallas import tpu as pltpu
from jax.sharding import PartitionSpec as P

MESH = pl.DeviceIdType.MESH
LOWEST = -1.0
CUTS = ((0, 80), (80, 80), (160, 96))
CHUNKS = len(CUTS)
STOPS = (
    (0, 0, 0),
    (1, 0, 0),
    (0, 1, 0),
    (1, 0, 1),
    (-1, 2, 0),
    (-1, -1, 0),
    (0, 2, 0),
    (-1, 0, 0),
    (0, 0, -1),
    (1, 0, 2),
    (0, 0, 2),
    (0, 0, 1),
    (-1, 1, 0),
)
(
    ENTER, NORMALIZE, OWN_KEYS, SEND, WAIT, SEND_KEYS, WAIT_KEYS, TWIN, WAIT_TWIN, TWIN_KEYS, WAIT_TWIN_KEYS, PREPARE, COMPARE, FINISH_ROWS, FINISH_COLS, TELL, HEAR, DRAIN, DRAIN_TWIN, DRAIN_TWIN_KEYS, DRAIN_TELL,
) = range(21)
PROGRAM = (
    (NORMALIZE, 0), (ENTER,), (SEND, 0, 0, 2, 2), (SEND, 0, 0, 11, 4), (SEND, 0, 0, 8, 5), (SEND, 0, 0, 7, 1),
    (SEND, 0, 0, 1, 0), (OWN_KEYS,), (TWIN_KEYS,), (TWIN, 0, 0), (NORMALIZE, 1), (TWIN, 0, 1), (NORMALIZE, 2),
    (TWIN, 0, 2), (SEND, 1, 0, 2, 2), (SEND, 2, 0, 7, 1), (SEND, 1, 0, 11, 4), (SEND, 1, 0, 1, 0), (SEND, 2, 0, 8, 5),
    (WAIT_TWIN_KEYS,), (SEND_KEYS, 0, 2, 2), (SEND_KEYS, 0, 11, 4), (SEND_KEYS, 0, 8, 5), (SEND_KEYS, 0, 7, 1),
    (SEND_KEYS, 0, 1, 0), (PREPARE, 0), (WAIT_TWIN, 0), (COMPARE, 0, 0, 2, True, True), (FINISH_ROWS, 0),
    (WAIT, 2, 0), (TWIN, 2, 0), (WAIT_KEYS, 2), (SEND_KEYS, 2, 6, 2), (PREPARE, 2), (WAIT, 11, 0), (TWIN, 11, 0),
    (WAIT_KEYS, 11), (SEND_KEYS, 11, 3, 0), (PREPARE, 11), (WAIT, 8, 0), (TWIN, 8, 0), (WAIT_KEYS, 8),
    (SEND_KEYS, 8, 10, 5), (PREPARE, 8), (WAIT, 7, 0), (TWIN, 7, 0), (WAIT_KEYS, 7), (SEND_KEYS, 7, 5, 3),
    (PREPARE, 7), (WAIT, 1, 0), (SEND, 0, 7, 5, 3), (SEND, 0, 2, 6, 2), (SEND, 2, 0, 11, 4), (SEND, 0, 11, 3, 0),
    (SEND, 1, 0, 7, 1), (SEND, 1, 0, 8, 5), (TWIN, 1, 0), (WAIT_KEYS, 1), (PREPARE, 1), (WAIT, 2, 1), (TWIN, 2, 1),
    (WAIT, 11, 1), (TWIN, 11, 1), (WAIT, 1, 1), (TWIN, 1, 1), (WAIT, 7, 2), (TWIN, 7, 2), (WAIT, 8, 2),
    (SEND, 2, 7, 5, 3), (SEND, 2, 0, 2, 2), (SEND, 2, 0, 1, 0), (SEND, 1, 2, 12, 1), (SEND, 1, 1, 3, 4),
    (SEND, 2, 8, 10, 5), (TWIN, 8, 2), (WAIT, 5, 0), (TWIN, 5, 0), (WAIT_KEYS, 5), (PREPARE, 5), (WAIT, 6, 0),
    (WAIT_KEYS, 6), (SEND_KEYS, 6, 4, 1), (PREPARE, 6), (WAIT, 3, 0), (TWIN, 3, 0), (WAIT_KEYS, 3),
    (SEND_KEYS, 3, 9, 4), (PREPARE, 3), (WAIT, 11, 2), (TWIN, 11, 2), (WAIT, 7, 1), (TWIN, 7, 1), (WAIT, 8, 1),
    (TWIN, 8, 1), (COMPARE, 7, 0, 0, True, True), (COMPARE, 11, 0, 3, True, False), (SEND, 1, 7, 5, 3),
    (SEND, 0, 3, 9, 4), (SEND, 0, 6, 4, 1), (SEND, 1, 2, 6, 2), (SEND, 2, 11, 3, 0), (COMPARE, 8, 0, 3, True, False),
    (SEND, 0, 8, 10, 5), (WAIT_TWIN, 11), (COMPARE, 8, 11, 1, True, True), (COMPARE, 7, 11, 0, False, True),
    (FINISH_ROWS, 7), (WAIT_TWIN, 7), (COMPARE, 8, 7, 0, False, True), (FINISH_ROWS, 8), (WAIT, 5, 2), (TWIN, 5, 2),
    (WAIT, 2, 2), (TWIN, 2, 2), (WAIT, 1, 2), (TWIN, 1, 2), (WAIT, 12, 1), (WAIT, 3, 1), (TWIN, 3, 1),
    (COMPARE, 1, 7, 1, True, False), (COMPARE, 2, 0, 0, True, False), (WAIT, 10, 2), (SEND, 2, 5, 4, 3),
    (SEND, 1, 12, 4, 2), (SEND, 2, 2, 12, 1), (SEND, 1, 3, 9, 4), (TWIN, 10, 2), (COMPARE, 2, 7, 0, False, False),
    (COMPARE, 2, 11, 0, False, False), (SEND, 2, 10, 9, 0), (SEND, 1, 8, 10, 5), (WAIT_TWIN, 8),
    (COMPARE, 2, 8, 0, False, True), (FINISH_ROWS, 2), (WAIT_TWIN, 2), (COMPARE, 1, 2, 0, False, True),
    (FINISH_ROWS, 1), (WAIT, 5, 1), (TWIN, 5, 1), (WAIT, 9, 0), (WAIT_KEYS, 9), (PREPARE, 9), (WAIT, 4, 0),
    (TWIN, 4, 0), (WAIT_KEYS, 4), (SEND_KEYS, 4, 12, 3), (PREPARE, 4), (WAIT, 6, 1), (COMPARE, 5, 11, 0, True, False),
    (COMPARE, 5, 8, 0, False, False), (WAIT, 3, 2), (TWIN, 3, 2), (WAIT, 10, 0), (SEND, 2, 2, 6, 2), (TWIN, 10, 0),
    (WAIT_KEYS, 10), (PREPARE, 10), (WAIT_TWIN, 1), (COMPARE, 5, 1, 0, False, True), (FINISH_COLS, 1, True),
    (TELL, 1, 0), (TELL, 1, 1), (COMPARE, 5, 2, 0, False, False), (FINISH_ROWS, 5), (SEND, 0, 4, 12, 3),
    (COMPARE, 3, 7, 0, True, False), (FINISH_COLS, 7, True), (TELL, 7, 0), (TELL, 7, 1),
    (COMPARE, 3, 8, 0, False, False), (COMPARE, 3, 2, 0, False, False), (WAIT_TWIN, 5),
    (COMPARE, 3, 5, 0, False, True), (FINISH_ROWS, 3), (WAIT, 4, 1), (TWIN, 4, 1), (WAIT, 9, 1), (WAIT, 4, 2),
    (TWIN, 4, 2), (WAIT, 12, 2), (WAIT, 10, 1), (TWIN, 10, 1), (COMPARE, 4, 11, 0, True, False), (WAIT_TWIN, 3),
    (COMPARE, 4, 3, 0, False, True), (WAIT, 9, 2), (COMPARE, 4, 8, 0, False, False), (COMPARE, 4, 1, 1, False, False),
    (FINISH_ROWS, 4), (COMPARE, 9, 5, 0, True, False), (COMPARE, 9, 2, 0, False, False),
    (COMPARE, 9, 7, 1, False, False), (WAIT_TWIN, 4), (COMPARE, 10, 4, 0, True, True), (FINISH_COLS, 4, True),
    (TELL, 4, 0), (TELL, 4, 1), (COMPARE, 9, 4, 1, False, False), (FINISH_ROWS, 9), (TELL, 9, 0),
    (COMPARE, 10, 5, 0, False, False), (FINISH_COLS, 5, True), (TELL, 5, 0), (TELL, 5, 1),
    (COMPARE, 10, 2, 0, False, False), (FINISH_COLS, 2, True), (TELL, 2, 0), (TELL, 2, 1), (FINISH_ROWS, 10),
    (TELL, 10, 0), (WAIT, 12, 0), (WAIT_KEYS, 12), (PREPARE, 12), (WAIT, 6, 2), (COMPARE, 12, 3, 0, True, False),
    (FINISH_COLS, 3, True), (TELL, 3, 0), (TELL, 3, 1), (COMPARE, 12, 8, 0, False, False), (FINISH_COLS, 8, True),
    (TELL, 8, 0), (TELL, 8, 1), (FINISH_ROWS, 12), (TELL, 12, 0), (COMPARE, 6, 11, 0, True, False),
    (FINISH_COLS, 11, False), (TELL, 11, 0), (TELL, 11, 1), (WAIT_TWIN, 10), (COMPARE, 6, 10, 1, False, True),
    (FINISH_ROWS, 6), (TELL, 6, 0), (COMPARE, 6, 0, 3, False, False), (FINISH_COLS, 0, True), (TELL, 0, 1),
    (DRAIN, 1), (DRAIN, 2), (DRAIN, 3), (DRAIN, 4), (DRAIN, 5), (DRAIN, 6), (DRAIN, 7), (DRAIN, 8), (DRAIN, 9),
    (DRAIN, 10), (DRAIN, 11), (DRAIN, 12), (DRAIN_TWIN, 0), (DRAIN_TWIN, 1), (DRAIN_TWIN, 2), (DRAIN_TWIN, 3),
    (DRAIN_TWIN, 4), (DRAIN_TWIN, 5), (DRAIN_TWIN, 7), (DRAIN_TWIN, 8), (DRAIN_TWIN, 10), (DRAIN_TWIN, 11),
    (DRAIN_TWIN_KEYS,), (HEAR, 1, 0), (HEAR, 1, 1), (HEAR, 7, 0), (HEAR, 7, 1), (HEAR, 4, 0), (HEAR, 4, 1),
    (HEAR, 9, 0), (HEAR, 5, 0), (HEAR, 5, 1), (HEAR, 2, 0), (HEAR, 2, 1), (HEAR, 10, 0), (HEAR, 3, 0), (HEAR, 3, 1),
    (HEAR, 8, 0), (HEAR, 8, 1), (HEAR, 12, 0), (HEAR, 11, 0), (HEAR, 11, 1), (HEAR, 6, 0), (HEAR, 0, 1),
    (DRAIN_TELL, 1, 0), (DRAIN_TELL, 1, 1), (DRAIN_TELL, 7, 0), (DRAIN_TELL, 7, 1), (DRAIN_TELL, 4, 0),
    (DRAIN_TELL, 4, 1), (DRAIN_TELL, 9, 0), (DRAIN_TELL, 5, 0), (DRAIN_TELL, 5, 1), (DRAIN_TELL, 2, 0),
    (DRAIN_TELL, 2, 1), (DRAIN_TELL, 10, 0), (DRAIN_TELL, 3, 0), (DRAIN_TELL, 3, 1), (DRAIN_TELL, 8, 0),
    (DRAIN_TELL, 8, 1), (DRAIN_TELL, 12, 0), (DRAIN_TELL, 11, 0), (DRAIN_TELL, 11, 1), (DRAIN_TELL, 6, 0),
    (DRAIN_TELL, 0, 1),
)
BOTH, ROWS, OWN, COLS = range(4)
STEPS_IN = ((1, 0, 0), (-1, 0, 0), (0, 1, 0), (0, -1, 0), (0, 0, 1), (0, 0, -1))
COUNT = len(STOPS)


def at_offset(offset, other_core):
    z, blk = lax.axis_index("grp"), lax.axis_index("blk")
    core, x, y = blk % 2, blk // 2 % 4, blk // 8
    if other_core:
        core = 1 - core
    x, y, z = (x + offset[0] + 4) % 4, (y + offset[1] + 4) % 4, (z + offset[2] + 4) % 4
    return (z, (y * 4 + x) * 2 + core)


def kernel(
    x_hbm, target_hbm, cluster_hbm, out_ref,
    raw, target, cluster, rows, keys, key_cols, row_max, col_max, parts, heard,
    copied, row_sent, row_got, key_sent, key_got, twin_sent, twin_got, twin_key, part_sent, part_got,
):
    size = raw.shape[0]
    here = (0, 0, 0)
    def piece(part):
        return pl.ds(CUTS[part][0], CUTS[part][1])

    def load(part):
        return pltpu.make_async_copy(x_hbm.at[piece(part)], raw.at[piece(part)], copied.at[part])

    load_target = pltpu.make_async_copy(target_hbm, target, copied.at[CHUNKS])
    load_cluster = pltpu.make_async_copy(cluster_hbm, cluster, copied.at[CHUNKS + 1])
    for part in range(CHUNKS):
        load(part).start()
    load_target.start()
    load_cluster.start()

    barrier = pltpu.get_barrier_semaphore()
    near = [at_offset(step, False) for step in STEPS_IN] + [at_offset(here, True)]
    for device in near:
        pl.semaphore_signal(barrier, inc=1, device_id=device, device_id_type=MESH)

    def normalize(part):
        load(part).wait()
        wide = raw[piece(part)].astype(jnp.float32)
        scale_inv = lax.rsqrt(jnp.sum(wide * wide, axis=1, keepdims=True) + 1e-06)
        rows[0, 0, piece(part)] = (wide * scale_inv).astype(jnp.bfloat16)

    def own_keys():
        load_target.wait()
        load_cluster.wait()
        key = jnp.right_shift(target[...], 5) * 64 + cluster[...]
        keys[0, 0] = key.astype(jnp.float32)

    def remote(src, dst, sent, got, device):
        return pltpu.make_async_remote_copy(
            src_ref=src, dst_ref=dst, send_sem=sent, recv_sem=got, device_id=device, device_id_type=MESH
        )

    def send_rows(part, src, dst, step):
        return remote(
            rows.at[src, 0, piece(part)], rows.at[dst, 0, piece(part)],
            row_sent.at[dst], row_got.at[dst, part], near[step],
        )

    def send_keys(src, dst, step):
        return remote(keys.at[src], keys.at[dst], key_sent.at[dst], key_got.at[dst], near[step])

    def to_twin(slot, where):
        return remote(rows.at[slot, 0, where], rows.at[slot, 1, where], twin_sent.at[slot], twin_got.at[slot], near[6])

    def keys_to_twin():
        return remote(keys.at[0, 0], keys.at[0, 1], twin_key.at[0], twin_key.at[1], near[6])

    def send_part(slot, half):
        offset = tuple(-v for v in STOPS[slot])
        return remote(
            parts.at[slot, half], heard.at[slot, half],
            part_sent.at[slot, half], part_got.at[slot, half], at_offset(offset, half == 1),
        )

    def prepare(slot):
        spread = jnp.broadcast_to(keys[slot, 0], (128, size))
        key_cols[slot] = spread.T

    def compare(left, right, mode, fresh_row, fresh_col):
        best_row = None
        for half in range(2):
            scores = lax.dot_general(
                rows[left, 0], rows[right, half], (((1,), (1,)), ((), ())), preferred_element_type=jnp.float32
            )
            for lane in range(0, size, 128):
                same = key_cols[left] == keys[right, half][:, lane : lane + 128]
                if mode == OWN and half == 0:
                    row_at = lax.broadcasted_iota(jnp.int32, (size, 128), 0)
                    col_at = lax.broadcasted_iota(jnp.int32, (size, 128), 1) + lane
                    same = same & (row_at != col_at)
                block = jnp.where(same, scores[:, lane : lane + 128], LOWEST)
                if mode != COLS:
                    best_row = block if best_row is None else jnp.maximum(best_row, block)
                if mode in (BOTH, COLS):
                    best = jnp.max(block.reshape(size // 8, 8, 128), axis=0)
                    place = (right, half, slice(None), slice(lane, lane + 128))
                    col_max[place] = best if fresh_col else jnp.maximum(col_max[place], best)
        if mode != COLS:
            row_max[left] = best_row if fresh_row else jnp.maximum(row_max[left], best_row)

    def finish_rows(slot):
        parts[slot, 0] = jnp.max(row_max[slot].T, axis=0, keepdims=True)

    def finish_cols(slot, add):
        col = jnp.max(col_max[slot, 0], axis=0, keepdims=True)
        parts[slot, 0] = jnp.maximum(parts[slot, 0], col) if add else col
        parts[slot, 1] = jnp.max(col_max[slot, 1], axis=0, keepdims=True)

    def drain(slot):
        remote(rows.at[0, 0], rows.at[slot, 0], row_sent.at[slot], row_got.at[slot, 0], near[0]).wait_send()
        send_keys(0, slot, 0).wait_send()

    whole = pl.ds(0, size)

    def run(program):
        best = None
        for op, *args in program:
            if op == ENTER:
                pl.semaphore_wait(barrier, len(near))
            elif op == NORMALIZE:
                normalize(*args)
            elif op == OWN_KEYS:
                own_keys()
            elif op == SEND:
                send_rows(*args).start()
            elif op == WAIT:
                send_rows(args[1], 0, args[0], 0).wait_recv()
            elif op == SEND_KEYS:
                send_keys(*args).start()
            elif op == WAIT_KEYS:
                send_keys(0, args[0], 0).wait_recv()
            elif op == TWIN:
                to_twin(args[0], piece(args[1])).start()
            elif op == WAIT_TWIN:
                to_twin(args[0], whole).wait_recv()
            elif op == TWIN_KEYS:
                keys_to_twin().start()
            elif op == WAIT_TWIN_KEYS:
                keys_to_twin().wait_recv()
            elif op == PREPARE:
                prepare(*args)
            elif op == COMPARE:
                compare(*args)
            elif op == FINISH_ROWS:
                finish_rows(*args)
            elif op == FINISH_COLS:
                finish_cols(*args)
            elif op == TELL:
                send_part(*args).start()
            elif op == HEAR:
                send_part(*args).wait_recv()
                news = heard[args[0], args[1]]
                best = news if best is None else jnp.maximum(best, news)
            elif op == DRAIN:
                drain(*args)
            elif op == DRAIN_TWIN:
                to_twin(args[0], whole).wait_send()
            elif op == DRAIN_TWIN_KEYS:
                keys_to_twin().wait_send()
            elif op == DRAIN_TELL:
                send_part(*args).wait_send()
        out_ref[...] = jnp.maximum(best, parts[0, 0])

    run(PROGRAM)


def body(embeddings, target, cluster):
    size, width = embeddings.shape
    hbm, vmem = pl.BlockSpec(memory_space=pltpu.HBM), pl.BlockSpec(memory_space=pltpu.VMEM)
    dma = pltpu.SemaphoreType.DMA
    best = pl.pallas_call(
        kernel,
        out_shape=jax.ShapeDtypeStruct((1, size), jnp.float32),
        in_specs=[hbm] * 3,
        out_specs=vmem,
        scratch_shapes=[
            pltpu.VMEM((size, width), jnp.bfloat16),
            pltpu.VMEM((1, size), jnp.int32),
            pltpu.VMEM((1, size), jnp.int32),
            pltpu.VMEM((COUNT, 2, size, width), jnp.bfloat16),
            pltpu.VMEM((COUNT, 2, 1, size), jnp.float32),
            pltpu.VMEM((COUNT, size, 128), jnp.float32),
            pltpu.VMEM((COUNT, size, 128), jnp.float32),
            pltpu.VMEM((COUNT, 2, 8, size), jnp.float32),
            pltpu.VMEM((COUNT, 2, 1, size), jnp.float32),
            pltpu.VMEM((COUNT, 2, 1, size), jnp.float32),
            dma((CHUNKS + 2,)), dma((COUNT,)), dma((COUNT, CHUNKS)), dma((COUNT,)), dma((COUNT,)),
            dma((COUNT,)), dma((COUNT,)), dma((2,)), dma((COUNT, 2)), dma((COUNT, 2)),
        ],
        compiler_params=pltpu.CompilerParams(
            collective_id=0, has_side_effects=True, vmem_limit_bytes=56553472
        ),
        name="nearest",
    )(embeddings, target.reshape(1, size), cluster.reshape(1, size))
    return best.reshape(size)


def solution(mesh):
    return jax.shard_map(
        body,
        mesh=mesh,
        in_specs=(P(("grp", "blk"), None), P(("grp", "blk"), None), P(("grp", "blk"))),
        out_specs=P(("grp", "blk")),
        check_vma=False,
    )
```
